256 devices in a mesh: col: 64 (over y, z, core), row: 4 (over x).
Axes of the slice: x: 4, y: 4, z: 8, core: 2. Of those that a mesh axis runs over, the one named last changes fastest.
Arguments:
- tiles: bfloat16 [1024, 6, 256, 256], P('col', None, 'row'), may hold values from 0.049804688 to 1
- tile_rows: int32 [1024, 6], P('col'), may hold values from 0 to 1023, as said below
- keep: int32 [1024, 6], P('col'), may hold values from 0 to 1, as said below
- hand: int32 [64], P('col'), may hold values from 0 to 8, as said below
Outputs:
- columns: bfloat16 [1024, 6, 256, 256], P('col', None, 'row')
The draws below stay inside these ranges and needn't reach their ends.
Inputs may be any that keep to these rules, and one draw needn't show every extreme that they name: `tile_rows`: slot 0 of column tile j is j itself; slots 1 to 3 are the other three column tiles of its aligned group of four on the same owner; slots 4 to 5 are column tiles of other owners, all distinct. The listing is symmetric: if k stands in slot s of j then j stands in slot s of k. For a k in slots 4 and up, the lists of j and k share only j and k. No owner lists more than (32 + 64 / 2 - 1) // (64 / 2) column tiles of one other owner, and some owner reaches that. `keep`: slot 0 is always kept. hand[d] equals hand[d + 64 / 2] for the first half of owners.
All inputs are finite; a program needn't handle non-finite values.
Results may differ from the reference program's by a relative error of at most 0.001.
Values may be sent and summed in bfloat16 or wider, within the bound.
A program may use at most 192 MiB of HBM per device.

```python
import math
import jax
import jax.numpy as jnp
from jax import lax

B = 256
REMOTE = 2
TILES_DEV = 16
SLOTS = 6
NT = 1024
N_COL = 64


def draw_tile_rows(key, part):
    key = jax.random.fold_in(key, 11)
    first_key, second_key = jax.random.split(key)
    relabel = jax.random.permutation(first_key, N_COL)
    inverse = jnp.argsort(relabel)
    offsets = 2 * jax.random.permutation(second_key, N_COL // 2) + 1
    device = jnp.arange(N_COL)[:, None]
    position = jnp.arange(TILES_DEV)[None, :]
    virtual = inverse[device]
    listed = [device * TILES_DEV + position + 0 * virtual]
    for flip in range(1, 4):
        listed.append(device * TILES_DEV + jnp.bitwise_xor(position, flip) + 0 * virtual)
    for match in range(REMOTE):
        shift_value = offsets[(position * REMOTE + match) % (N_COL // 2)]
        other = relabel[(shift_value - virtual) % N_COL]
        listed.append(other * TILES_DEV + position)
    return jnp.stack(listed, -1).reshape(NT, SLOTS).astype(jnp.int32)


def draw_keep(key, part):
    key = jax.random.fold_in(key, 12)
    first_key, second_key = jax.random.split(key)
    levels = jax.random.randint(first_key, (N_COL, 1, 1), 1, 5)
    rolled = jax.random.randint(second_key, (N_COL, TILES_DEV, SLOTS), 0, 4)
    kept = (rolled < levels).astype(jnp.int32)
    first_slot = jnp.arange(SLOTS)[None, None, :] == 0
    kept = jnp.where(first_slot, 1, kept)
    return kept.reshape(NT, SLOTS).astype(jnp.int32)


def draw_hand(key, part):
    key = jax.random.fold_in(key, 13)
    counts = jax.random.randint(key, (N_COL // 2,), 0, TILES_DEV // 2 + 1)
    counts = counts.at[0].set(TILES_DEV // 2)
    return jnp.concatenate([counts, counts]).astype(jnp.int32)


def shard_levels(stream_key, extent, pieces, low, largest):
    loudness = 1.0
    for dim, parts in pieces:
        steps = jax.random.uniform(jax.random.fold_in(jax.random.fold_in(stream_key, 6), dim), (parts,), jnp.float32, low / len(pieces), largest / len(pieces))
        loudness = loudness * jnp.repeat(jnp.exp(steps), extent[dim] // parts).reshape((-1,) + (1,) * (len(extent) - 1 - dim))
    return loudness


def setup_inputs(seed: int = 0) -> dict:
    arg_keys = jax.random.split(jax.random.key(seed), 5)
    tiles = jnp.clip(jnp.exp(math.log(1.0) - 2.9996462 * jax.random.uniform(arg_keys[0], (NT, SLOTS, B, B), jnp.float32) ** shard_levels(arg_keys[0], (NT, SLOTS, B, B), ((0, 64), (2, 4)), -0.2, 0.2)), 0.049804688, 1.0).astype(jnp.bfloat16)
    tile_rows = draw_tile_rows(jax.random.fold_in(arg_keys[4], 71), 0)
    keep = draw_keep(jax.random.fold_in(arg_keys[4], 71), 0)
    hand = draw_hand(jax.random.fold_in(arg_keys[4], 71), 0)
    return dict(tiles=tiles, tile_rows=tile_rows, keep=keep, hand=hand)


def reference(tiles, tile_rows, keep, hand):
    def one_column(index):
        listed = tile_rows[index]
        near = tiles[listed].astype(jnp.float32)
        near_rows = tile_rows[listed]
        match = (near_rows[:, :, None] == listed[None, None, :]).astype(jnp.float32)
        picked = jnp.einsum('stq,stab->qsab', match, near)
        own = tiles[index].astype(jnp.float32)
        expanded = jnp.einsum('qsab,sbc->qac', picked, own)
        expanded = expanded * keep[index].astype(jnp.float32)[:, None, None]
        inflated = expanded * expanded
        column_sum = jnp.sum(inflated, axis=(0, 1))
        return (B * inflated / column_sum[None, None, :]).astype(jnp.bfloat16)

    state = lax.map(one_column, jnp.arange(NT, dtype=jnp.int32))
    state = state.reshape(N_COL, TILES_DEV, SLOTS, B, B)
    partner = jnp.roll(state, -(N_COL // 2), axis=0)
    position = jnp.arange(TILES_DEV, dtype=jnp.int32)[None, :]
    handed = position >= (TILES_DEV - hand)[:, None]
    result = jnp.where(handed[:, :, None, None, None], partner, state)
    return result.reshape(NT, SLOTS, B, B)
```

```python
import functools

import jax
import jax.numpy as jnp
from jax import lax
from jax.experimental import pallas as pl
from jax.experimental.pallas import tpu as pltpu
from jax.sharding import PartitionSpec as P

MESH = pl.DeviceIdType.MESH
NEAR = 4
STRIDE = 27
LEVELS = 32767.0


def coded(e):
    top = jnp.maximum(jnp.max(e, axis=0, keepdims=True), 1e-30)
    code = (e * (LEVELS / top) + 0.5).astype(jnp.int32).astype(jnp.int16)
    step = top * (1.0 / LEVELS)
    return code, step * step


def squared(code):
    value = code.astype(jnp.int32).astype(jnp.float32)
    return value * value


def kernel(
    n,
    rows_ref,
    keep_ref,
    hand_ref,
    slot_ref,
    tiles_ref,
    out_ref,
    full,
    stage,
    arrived_a,
    arrived_b,
    acc,
    sums,
    sums_in,
    steps,
    factors,
    factors_in,
    early,
    early_in,
    late,
    late_in,
    x_send,
    x_recv,
    z_send,
    z_recv,
    s_send,
    s_recv,
    h_send,
    h_recv,
):
    count, slots, height, width = tiles_ref.shape
    arrived = (arrived_a, arrived_b)
    half = count // 2
    part = height // 2
    me = lax.axis_index("col")
    x = lax.axis_index("row")
    up, down, across = lax.rem(x + 1, 4), lax.rem(x + 3, 4), lax.rem(x + 2, 4)
    partner = lax.rem(me + n // 2, n)
    mixed = (0,) + tuple(range(NEAR, slots))
    lag = 2
    ahead = 4
    pairs = count // 2
    groups = count // NEAR
    per = 2 * n // pairs

    barrier = pltpu.get_barrier_semaphore()
    for peer in (up, down, across):
        pl.semaphore_signal(barrier, inc=1, device_id={"row": peer}, device_id_type=MESH)

    @pl.loop(1, n)
    def _(t):
        pl.semaphore_signal(
            barrier, inc=1, device_id={"col": lax.rem(me + t, n)}, device_id_type=MESH
        )

    sums[...] = jnp.zeros_like(sums)
    factors[...] = jnp.zeros_like(factors)
    pl.semaphore_wait(barrier, n + 2)

    def direct(j, way):
        return pltpu.make_async_remote_copy(
            src_ref=tiles_ref.at[j],
            dst_ref=full.at[j, x],
            send_sem=x_send.at[way, j],
            recv_sem=x_recv.at[way, j],
            device_id={"row": (up, down)[way]},
            device_id_type=MESH,
        )

    def relay(j, way):
        origin = (down, up)[way]
        return pltpu.make_async_remote_copy(
            src_ref=full.at[j, origin],
            dst_ref=full.at[j, origin],
            send_sem=x_send.at[2, j],
            recv_sem=x_recv.at[2, j],
            device_id={"row": (up, down)[way]},
            device_id_type=MESH,
        )

    def far(h, t):
        return pltpu.make_async_remote_copy(
            src_ref=stage.at[h, t - 1],
            dst_ref=arrived[h].at[t - 1],
            send_sem=z_send.at[h, t - 1],
            recv_sem=z_recv.at[h, t - 1],
            device_id={"col": lax.rem(me + t, n)},
            device_id_type=MESH,
        )

    def total(g, k):
        return pltpu.make_async_remote_copy(
            src_ref=sums.at[g],
            dst_ref=sums_in.at[k, g],
            send_sem=s_send.at[g, k],
            recv_sem=s_recv.at[g, k],
            device_id={"row": (up, down, across)[k]},
            device_id_type=MESH,
        )

    def to_partner(source, target, kind, i):
        return pltpu.make_async_remote_copy(
            src_ref=source,
            dst_ref=target,
            send_sem=h_send.at[kind, i],
            recv_sem=h_recv.at[kind, i],
            device_id={"col": partner},
            device_id_type=MESH,
        )

    def hand_late(h, j):
        return to_partner(late.at[h, j - half], late_in.at[h, j - half], h, j - half)

    def hand_early(j):
        return to_partner(early.at[j - half], early_in.at[j - half], 2, j - half)

    def hand_factor(j):
        return to_partner(factors.at[j - half], factors_in.at[j - half], 3, j - half)

    def send_far(number):
        i = lax.rem(number, n)
        t = lax.rem(i * STRIDE, n)
        pick = slot_ref[t]
        column = lax.rem(pick, count)
        for h in range(2):

            @pl.when((i > 0) & (number // n == h))
            def _():
                rows = pl.ds(h * part, part)
                stage[h, t - 1, 0] = tiles_ref[column, 0, rows]
                stage[h, t - 1, 1] = tiles_ref[column, NEAR + pick // count, rows]
                far(h, t).start()

    @pl.loop(0, lag)
    def _(p):
        for k in range(2):
            for way in range(2):
                direct(count - 1 - k - 2 * p, way).start()

                @pl.loop(0, per // 4)
                def _(m):
                    send_far(p * per + (2 * k + way) * (per // 4) + m)

    @pl.loop(lag * per, ahead * per)
    def _(number):
        send_far(number)

    @pl.loop(0, count)
    def _(j):
        full[j, x] = tiles_ref[j]

    def right(j, s):
        return full[j, :, s].reshape(4 * height, width)

    def row_of(ref, j):
        return ref[j // NEAR, pl.ds(lax.rem(j, NEAR), 1), :]

    def set_row(ref, j, value):
        ref[j // NEAR, pl.ds(lax.rem(j, NEAR), 1), :] = value

    def near(j, hands):
        left = []
        for s in range(NEAR):
            column = j if s == 0 else lax.rem(rows_ref[s, j], count)
            left.append(
                jnp.concatenate([tiles_ref[column, q ^ s] for q in range(NEAR)], axis=0)
            )
        a = jnp.concatenate(left, axis=1)
        b = jnp.concatenate([right(j, s) for s in range(NEAR)], axis=0)
        p = jnp.dot(a, b, preferred_element_type=jnp.float32).reshape(NEAR, height, width)
        acc[j, 0] = p[0]
        column_sum = jnp.zeros((1, width), jnp.float32)
        for q in range(1, NEAR):
            e = p[q] * keep_ref[q, j].astype(jnp.float32)
            if hands:
                early[j - half, q - 1], step = coded(e)
                steps[j - half, q - 1 : q, :] = step
            e = e * e
            acc[j, q] = e
            column_sum = column_sum + jnp.sum(e, axis=0, keepdims=True)
        set_row(sums, j, column_sum)
        c = tiles_ref[j, NEAR:].reshape((slots - NEAR) * height, width)
        acc[j, NEAR:] = jnp.dot(c, right(j, 0), preferred_element_type=jnp.float32).reshape(
            slots - NEAR, height, width
        )
        if hands:
            hand_early(j).start()

    def expand(h, columns, hands):
        rows = pl.ds(h * part, part)
        products = []
        for j in columns:
            for s in range(NEAR, slots):
                t = lax.rem(me - rows_ref[s, j] // count + n, n)
                a = arrived[h][jnp.maximum(t - 1, 0)].reshape(2 * part, width)
                products.append(
                    jnp.dot(a, right(j, s), preferred_element_type=jnp.float32)
                )
        for c, j in enumerate(columns):
            mine = products[c * (slots - NEAR) : (c + 1) * (slots - NEAR)]
            own = acc[j, 0, rows]
            for p in mine:
                own = own + p[part:]
            values = [own] + [acc[j, NEAR + i, rows] + p[:part] for i, p in enumerate(mine)]
            column_sum = row_of(sums, j)
            for i, q in enumerate(mixed):
                e = values[i] * keep_ref[q, j].astype(jnp.float32)
                if hands:
                    late[h, j - half, i], step = coded(e)
                    r = NEAR - 1 + h * len(mixed) + i
                    steps[j - half, r : r + 1, :] = step
                e = e * e
                acc[j, q, rows] = e
                column_sum = column_sum + jnp.sum(e, axis=0, keepdims=True)
            set_row(sums, j, column_sum)
            if hands:
                hand_late(h, j).start()

    def scale_of(j):
        whole = row_of(sums, j)
        for k in range(3):
            whole = whole + row_of(sums_in.at[k], j)
        return width / whole

    def pass_on(p):
        for k in range(2):
            j = count - 1 - k - 2 * p
            direct(j, k).wait_recv()
            relay(j, k).start()
            for way in range(2):

                @pl.when(p + lag < pairs)
                def _():
                    direct(j - 2 * lag, way).start()

                @pl.loop(0, per // 4)
                def _(m):
                    send_far((p + ahead) * per + (2 * k + way) * (per // 4) + m)

    def near_pair(p, hands):
        for k in range(2):
            j = count - 1 - k - 2 * p
            direct(j, 1 - k).wait_recv()
            relay(j, k).wait_recv()
            near(j, hands)

    def await_far(h):
        @pl.loop(1, n)
        def _(t):
            far(h, t).wait_recv()

    def expand_all(h, first, last, hands):
        @pl.loop(0, (last - first) // 2)
        def _(i):
            j = last - 1 - 2 * i
            expand(h, (j, j - 1), hands)

    def start_totals(g):
        for k in range(3):
            total(g, k).start()

    def await_totals(g):
        for k in range(3):
            total(g, k).wait_recv()

    def normalize(g):
        await_totals(g)

        @pl.loop(g * NEAR, (g + 1) * NEAR)
        def _(j):
            scale = scale_of(j)
            for q in range(slots):
                out_ref[j, q] = (acc[j, q] * scale).astype(jnp.bfloat16)

    @pl.loop(0, lag)
    def _(p):
        pass_on(p)

    @pl.loop(lag, pairs // 2 + lag)
    def _(p):
        pass_on(p)
        near_pair(p - lag, True)

    pass_on(pairs // 2 + lag)
    await_far(0)
    expand_all(0, half, count, True)
    near_pair(pairs // 2, False)
    pass_on(pairs // 2 + lag + 1)
    near_pair(pairs // 2 + 1, False)
    expand_all(0, NEAR, 2 * NEAR, False)

    await_far(1)
    for g in (3, 2, 1):
        expand_all(1, g * NEAR, (g + 1) * NEAR, g > 1)
        start_totals(g)

    for g in (3, 2):
        await_totals(g)

        @pl.loop(g * NEAR, (g + 1) * NEAR)
        def _(j):
            scale = scale_of(j)
            for r in range(NEAR - 1 + 2 * len(mixed)):
                factors[j - half, r : r + 1, :] = steps[j - half, r : r + 1, :] * scale
            hand_factor(j).start()

    @pl.loop(pairs // 2 + 2, pairs)
    def _(p):
        near_pair(p, False)

    expand_all(0, 0, NEAR, False)
    expand_all(1, 0, NEAR, False)
    start_totals(0)
    normalize(1)

    first = count - hand_ref[0]

    @pl.loop(0, half)
    def _(i):
        j = count - 1 - i
        hand_factor(j).wait_recv()
        hand_early(j).wait_recv()
        for h in range(2):
            hand_late(h, j).wait_recv()
        scale = scale_of(j)
        take = jnp.full((height, width), j, jnp.int32) >= first
        for q in range(1, NEAR):
            theirs = squared(early_in[j - half, q - 1]) * factors_in[j - half, q - 1 : q, :]
            out_ref[j, q] = jnp.where(take, theirs, acc[j, q] * scale).astype(jnp.bfloat16)
        for i, q in enumerate(mixed):
            for h in range(2):
                rows = pl.ds(h * part, part)
                r = NEAR - 1 + h * len(mixed) + i
                theirs = squared(late_in[h, j - half, i]) * factors_in[j - half, r : r + 1, :]
                out_ref[j, q, rows] = jnp.where(
                    take[:part], theirs, acc[j, q, rows] * scale
                ).astype(jnp.bfloat16)

    normalize(0)

    @pl.loop(0, count)
    def _(j):
        for way in range(2):
            direct(j, way).wait_send()

    @pl.loop(0, pairs)
    def _(p):
        for k in range(2):
            relay(count - 1 - k - 2 * p, k).wait_send()

    @pl.loop(1, n)
    def _(t):
        for h in range(2):
            far(h, t).wait_send()

    @pl.loop(half, count)
    def _(j):
        hand_early(j).wait_send()
        hand_factor(j).wait_send()
        for h in range(2):
            hand_late(h, j).wait_send()

    for g in range(groups):
        for k in range(3):
            total(g, k).wait_send()


def local(n, tiles, tile_rows, keep, hand):
    count, slots, height, width = tiles.shape
    half = count // 2
    part = height // 2
    groups = count // NEAR
    far_count = slots - NEAR
    me = lax.axis_index("col")
    tile_rows = tile_rows.T
    owner = tile_rows[NEAR:] // count
    shift = (owner - me + n) % n
    request = jnp.arange(far_count * count, dtype=jnp.int32).reshape(far_count, count)
    turn = jnp.arange(n, dtype=jnp.int32)[:, None, None]
    slot = jnp.sum(jnp.where(shift[None] == turn, request[None], 0), (1, 2))
    smem = pl.BlockSpec(memory_space=pltpu.SMEM)
    vmem = pl.BlockSpec(memory_space=pltpu.VMEM)
    dma = pltpu.SemaphoreType.DMA
    return pl.pallas_call(
        functools.partial(kernel, n),
        out_shape=pltpu.VMEM(tiles.shape, tiles.dtype),
        in_specs=[smem, smem, smem, smem, vmem],
        out_specs=vmem,
        scratch_shapes=[
            pltpu.VMEM((count, 4, slots, height, width), jnp.bfloat16),
            pltpu.VMEM((2, n - 1, 2, part, width), jnp.bfloat16),
            pltpu.VMEM((n - 1, 2, part, width), jnp.bfloat16),
            pltpu.VMEM((n - 1, 2, part, width), jnp.bfloat16),
            pltpu.VMEM((count, slots, height, width), jnp.float32),
            pltpu.VMEM((groups, 8, width), jnp.float32),
            pltpu.VMEM((3, groups, 8, width), jnp.float32),
            pltpu.VMEM((half, 16, width), jnp.float32),
            pltpu.VMEM((half, 16, width), jnp.float32),
            pltpu.VMEM((half, 16, width), jnp.float32),
            pltpu.VMEM((half, NEAR - 1, height, width), jnp.int16),
            pltpu.VMEM((half, NEAR - 1, height, width), jnp.int16),
            pltpu.VMEM((2, half, 1 + far_count, part, width), jnp.int16),
            pltpu.VMEM((2, half, 1 + far_count, part, width), jnp.int16),
            dma((3, count)),
            dma((3, count)),
            dma((2, n - 1)),
            dma((2, n - 1)),
            dma((groups, 3)),
            dma((groups, 3)),
            dma((4, half)),
            dma((4, half)),
        ],
        compiler_params=pltpu.CompilerParams(
            collective_id=0, has_side_effects=True, vmem_limit_bytes=56 * 1024 * 1024
        ),
        cost_estimate=pl.CostEstimate(
            flops=22 * 2 * count * height * 4 * height * width,
            bytes_accessed=2 * tiles.size * 2,
            transcendentals=0,
        ),
    )(tile_rows, keep.T, hand, slot, tiles)


def solution(mesh):
    placed = (P("col", None, "row", None), P("col", None), P("col", None), P("col"))
    return jax.shard_map(
        functools.partial(local, mesh.shape["col"]),
        mesh=mesh,
        in_specs=placed,
        out_specs=P("col", None, "row", None),
        check_vma=False,
    )
```

```python
import functools

import jax
import jax.numpy as jnp
from jax import lax
from jax.experimental import pallas as pl
from jax.experimental.pallas import tpu as pltpu
from jax.sharding import PartitionSpec as P

MESH = pl.DeviceIdType.MESH
NEAR = 4
STRIDE = 27
LEVELS = 32767.0


def coded(e):
    top = jnp.maximum(jnp.max(e, axis=0, keepdims=True), 1e-30)
    code = (e * (LEVELS / top) + 0.5).astype(jnp.int32).astype(jnp.int16)
    step = top * (1.0 / LEVELS)
    return code, step * step


def squared(code):
    value = code.astype(jnp.int32).astype(jnp.float32)
    return value * value


def kernel(
    n,
    rows_ref,
    keep_ref,
    hand_ref,
    slot_ref,
    source_ref,
    out_ref,
    tiles_ref,
    full,
    stage,
    arrived_a,
    arrived_b,
    acc,
    sums,
    sums_in,
    steps,
    factors,
    factors_in,
    early,
    early_in,
    late,
    late_in,
    x_send,
    x_recv,
    z_send,
    z_recv,
    s_send,
    s_recv,
    h_send,
    h_recv,
    own_sem,
):
    count, slots, height, width = tiles_ref.shape
    arrived = (arrived_a, arrived_b)
    half = count // 2
    part = height // 2
    me = lax.axis_index("col")
    x = lax.axis_index("row")
    up, down, across = lax.rem(x + 1, 4), lax.rem(x + 3, 4), lax.rem(x + 2, 4)
    partner = lax.rem(me + n // 2, n)
    mixed = (0,) + tuple(range(NEAR, slots))
    lag = 2
    ahead = 2
    pairs = count // 2
    groups = count // NEAR
    per = 2 * n // pairs

    held = pltpu.make_async_copy(source_ref, tiles_ref, own_sem.at[0])
    held.start()
    placed = pltpu.make_async_copy(source_ref, full.at[:, x], own_sem.at[1])
    placed.start()

    barrier = pltpu.get_barrier_semaphore()
    for peer in (up, down, across):
        pl.semaphore_signal(barrier, inc=1, device_id={"row": peer}, device_id_type=MESH)

    @pl.loop(1, n)
    def _(t):
        pl.semaphore_signal(
            barrier, inc=1, device_id={"col": lax.rem(me + t, n)}, device_id_type=MESH
        )

    sums[...] = jnp.zeros_like(sums)
    factors[...] = jnp.zeros_like(factors)
    held.wait()
    pl.semaphore_wait(barrier, n + 2)

    def direct(j, way):
        return pltpu.make_async_remote_copy(
            src_ref=tiles_ref.at[j],
            dst_ref=full.at[j, x],
            send_sem=x_send.at[way, j],
            recv_sem=x_recv.at[way, j],
            device_id={"row": (up, down)[way]},
            device_id_type=MESH,
        )

    def relay(j, way):
        origin = (down, up)[way]
        return pltpu.make_async_remote_copy(
            src_ref=full.at[j, origin],
            dst_ref=full.at[j, origin],
            send_sem=x_send.at[2, j],
            recv_sem=x_recv.at[2, j],
            device_id={"row": (up, down)[way]},
            device_id_type=MESH,
        )

    def far(h, t):
        return pltpu.make_async_remote_copy(
            src_ref=stage.at[h, t - 1],
            dst_ref=arrived[h].at[t - 1],
            send_sem=z_send.at[h, t - 1],
            recv_sem=z_recv.at[h, t - 1],
            device_id={"col": lax.rem(me + t, n)},
            device_id_type=MESH,
        )

    def total(g, k):
        return pltpu.make_async_remote_copy(
            src_ref=sums.at[g],
            dst_ref=sums_in.at[k, g],
            send_sem=s_send.at[g, k],
            recv_sem=s_recv.at[g, k],
            device_id={"row": (up, down, across)[k]},
            device_id_type=MESH,
        )

    def to_partner(source, target, kind, i):
        return pltpu.make_async_remote_copy(
            src_ref=source,
            dst_ref=target,
            send_sem=h_send.at[kind, i],
            recv_sem=h_recv.at[kind, i],
            device_id={"col": partner},
            device_id_type=MESH,
        )

    def hand_late(h, j):
        return to_partner(late.at[h, j - half], late_in.at[h, j - half], h, j - half)

    def hand_early(j):
        return to_partner(early.at[j - half], early_in.at[j - half], 2, j - half)

    def hand_factor(j):
        return to_partner(factors.at[j - half], factors_in.at[j - half], 3, j - half)

    def send_far(number):
        i = lax.rem(number, n)
        t = lax.rem(i * STRIDE, n)
        pick = slot_ref[t]
        column = lax.rem(pick, count)
        for h in range(2):

            @pl.when((i > 0) & (number // n == h))
            def _():
                rows = pl.ds(h * part, part)
                stage[h, t - 1, 0] = tiles_ref[column, 0, rows]
                stage[h, t - 1, 1] = tiles_ref[column, NEAR + pick // count, rows]
                far(h, t).start()

    @pl.loop(0, lag)
    def _(p):
        for k in range(2):
            for way in range(2):
                direct(count - 1 - k - 2 * p, way).start()

                @pl.loop(0, per // 4)
                def _(m):
                    send_far(p * per + (2 * k + way) * (per // 4) + m)

    @pl.loop(lag * per, ahead * per)
    def _(number):
        send_far(number)

    placed.wait()

    def right(j, s):
        return full[j, :, s].reshape(4 * height, width)

    def row_of(ref, j):
        return ref[j // NEAR, pl.ds(lax.rem(j, NEAR), 1), :]

    def set_row(ref, j, value):
        ref[j // NEAR, pl.ds(lax.rem(j, NEAR), 1), :] = value

    def near(j, hands):
        left = []
        for s in range(NEAR):
            column = j if s == 0 else lax.rem(rows_ref[s, j], count)
            left.append(
                jnp.concatenate([tiles_ref[column, q ^ s] for q in range(NEAR)], axis=0)
            )
        a = jnp.concatenate(left, axis=1)
        b = jnp.concatenate([right(j, s) for s in range(NEAR)], axis=0)
        p = jnp.dot(a, b, preferred_element_type=jnp.float32).reshape(NEAR, height, width)
        acc[j, 0] = p[0]
        column_sum = jnp.zeros((1, width), jnp.float32)
        for q in range(1, NEAR):
            e = p[q] * keep_ref[q, j].astype(jnp.float32)
            if hands:
                early[j - half, q - 1], step = coded(e)
                steps[j - half, q - 1 : q, :] = step
            e = e * e
            acc[j, q] = e
            column_sum = column_sum + jnp.sum(e, axis=0, keepdims=True)
        set_row(sums, j, column_sum)
        c = tiles_ref[j, NEAR:].reshape((slots - NEAR) * height, width)
        acc[j, NEAR:] = jnp.dot(c, right(j, 0), preferred_element_type=jnp.float32).reshape(
            slots - NEAR, height, width
        )
        if hands:
            hand_early(j).start()

    def expand(h, columns, hands):
        rows = pl.ds(h * part, part)
        products = []
        for j in columns:
            for s in range(NEAR, slots):
                t = lax.rem(me - rows_ref[s, j] // count + n, n)
                a = arrived[h][jnp.maximum(t - 1, 0)].reshape(2 * part, width)
                products.append(
                    jnp.dot(a, right(j, s), preferred_element_type=jnp.float32)
                )
        for c, j in enumerate(columns):
            mine = products[c * (slots - NEAR) : (c + 1) * (slots - NEAR)]
            own = acc[j, 0, rows]
            for p in mine:
                own = own + p[part:]
            values = [own] + [acc[j, NEAR + i, rows] + p[:part] for i, p in enumerate(mine)]
            column_sum = row_of(sums, j)
            for i, q in enumerate(mixed):
                e = values[i] * keep_ref[q, j].astype(jnp.float32)
                if hands:
                    late[h, j - half, i], step = coded(e)
                    r = NEAR - 1 + h * len(mixed) + i
                    steps[j - half, r : r + 1, :] = step
                e = e * e
                acc[j, q, rows] = e
                column_sum = column_sum + jnp.sum(e, axis=0, keepdims=True)
            set_row(sums, j, column_sum)
            if hands:
                hand_late(h, j).start()

    def scale_of(j):
        whole = row_of(sums, j)
        for k in range(3):
            whole = whole + row_of(sums_in.at[k], j)
        return width / whole

    def pass_on(p):
        for k in range(2):
            j = count - 1 - k - 2 * p
            direct(j, k).wait_recv()
            relay(j, k).start()
            for way in range(2):

                @pl.when(p + lag < pairs)
                def _():
                    direct(j - 2 * lag, way).start()

                @pl.loop(0, per // 4)
                def _(m):
                    send_far((p + ahead) * per + (2 * k + way) * (per // 4) + m)

    def near_pair(p, hands):
        for k in range(2):
            j = count - 1 - k - 2 * p
            direct(j, 1 - k).wait_recv()
            relay(j, k).wait_recv()
            near(j, hands)

    def await_far(h):
        @pl.loop(1, n)
        def _(t):
            far(h, t).wait_recv()

    def expand_all(h, first, last, hands):
        @pl.loop(0, (last - first) // 2)
        def _(i):
            j = last - 1 - 2 * i
            expand(h, (j, j - 1), hands)

    def start_totals(g):
        for k in range(3):
            total(g, k).start()

    def await_totals(g):
        for k in range(3):
            total(g, k).wait_recv()

    def normalize(g):
        await_totals(g)

        @pl.loop(g * NEAR, (g + 1) * NEAR)
        def _(j):
            scale = scale_of(j)
            for q in range(slots):
                out_ref[j, q] = (acc[j, q] * scale).astype(jnp.bfloat16)

    @pl.loop(0, lag)
    def _(p):
        pass_on(p)

    @pl.loop(lag, pairs // 2 + lag)
    def _(p):
        pass_on(p)
        near_pair(p - lag, True)

    pass_on(pairs // 2 + lag)
    await_far(0)
    expand_all(0, half, count, True)
    near_pair(pairs // 2, False)
    pass_on(pairs // 2 + lag + 1)
    near_pair(pairs // 2 + 1, False)
    expand_all(0, NEAR, 2 * NEAR, False)

    await_far(1)
    for g in (3, 2, 1):
        expand_all(1, g * NEAR, (g + 1) * NEAR, g > 1)
        start_totals(g)

    for g in (3, 2):
        await_totals(g)

        @pl.loop(g * NEAR, (g + 1) * NEAR)
        def _(j):
            scale = scale_of(j)
            for r in range(NEAR - 1 + 2 * len(mixed)):
                factors[j - half, r : r + 1, :] = steps[j - half, r : r + 1, :] * scale
            hand_factor(j).start()

    @pl.loop(pairs // 2 + 2, pairs)
    def _(p):
        near_pair(p, False)

    expand_all(0, 0, NEAR, False)
    expand_all(1, 0, NEAR, False)
    start_totals(0)
    normalize(1)

    first = count - hand_ref[0]

    @pl.loop(0, half)
    def _(i):
        j = count - 1 - i
        hand_factor(j).wait_recv()
        hand_early(j).wait_recv()
        for h in range(2):
            hand_late(h, j).wait_recv()
        scale = scale_of(j)
        take = jnp.full((height, width), j, jnp.int32) >= first
        for q in range(1, NEAR):
            theirs = squared(early_in[j - half, q - 1]) * factors_in[j - half, q - 1 : q, :]
            out_ref[j, q] = jnp.where(take, theirs, acc[j, q] * scale).astype(jnp.bfloat16)
        for i, q in enumerate(mixed):
            for h in range(2):
                rows = pl.ds(h * part, part)
                r = NEAR - 1 + h * len(mixed) + i
                theirs = squared(late_in[h, j - half, i]) * factors_in[j - half, r : r + 1, :]
                out_ref[j, q, rows] = jnp.where(
                    take[:part], theirs, acc[j, q, rows] * scale
                ).astype(jnp.bfloat16)

    normalize(0)

    @pl.loop(0, count)
    def _(j):
        for way in range(2):
            direct(j, way).wait_send()

    @pl.loop(0, pairs)
    def _(p):
        for k in range(2):
            relay(count - 1 - k - 2 * p, k).wait_send()

    @pl.loop(1, n)
    def _(t):
        for h in range(2):
            far(h, t).wait_send()

    @pl.loop(half, count)
    def _(j):
        hand_early(j).wait_send()
        hand_factor(j).wait_send()
        for h in range(2):
            hand_late(h, j).wait_send()

    for g in range(groups):
        for k in range(3):
            total(g, k).wait_send()


def local(n, tiles, tile_rows, keep, hand):
    count, slots, height, width = tiles.shape
    half = count // 2
    part = height // 2
    groups = count // NEAR
    far_count = slots - NEAR
    me = lax.axis_index("col")
    tile_rows = tile_rows.T
    owner = tile_rows[NEAR:] // count
    shift = (owner - me + n) % n
    request = jnp.arange(far_count * count, dtype=jnp.int32).reshape(far_count, count)
    turn = jnp.arange(n, dtype=jnp.int32)[:, None, None]
    slot = jnp.sum(jnp.where(shift[None] == turn, request[None], 0), (1, 2))
    smem = pl.BlockSpec(memory_space=pltpu.SMEM)
    vmem = pl.BlockSpec(memory_space=pltpu.VMEM)
    dma = pltpu.SemaphoreType.DMA
    return pl.pallas_call(
        functools.partial(kernel, n),
        out_shape=pltpu.VMEM(tiles.shape, tiles.dtype),
        in_specs=[smem, smem, smem, smem, pl.BlockSpec(memory_space=pl.ANY)],
        out_specs=vmem,
        scratch_shapes=[
            pltpu.VMEM(tiles.shape, tiles.dtype),
            pltpu.VMEM((count, 4, slots, height, width), jnp.bfloat16),
            pltpu.VMEM((2, n - 1, 2, part, width), jnp.bfloat16),
            pltpu.VMEM((n - 1, 2, part, width), jnp.bfloat16),
            pltpu.VMEM((n - 1, 2, part, width), jnp.bfloat16),
            pltpu.VMEM((count, slots, height, width), jnp.float32),
            pltpu.VMEM((groups, 8, width), jnp.float32),
            pltpu.VMEM((3, groups, 8, width), jnp.float32),
            pltpu.VMEM((half, 16, width), jnp.float32),
            pltpu.VMEM((half, 16, width), jnp.float32),
            pltpu.VMEM((half, 16, width), jnp.float32),
            pltpu.VMEM((half, NEAR - 1, height, width), jnp.int16),
            pltpu.VMEM((half, NEAR - 1, height, width), jnp.int16),
            pltpu.VMEM((2, half, 1 + far_count, part, width), jnp.int16),
            pltpu.VMEM((2, half, 1 + far_count, part, width), jnp.int16),
            dma((3, count)),
            dma((3, count)),
            dma((2, n - 1)),
            dma((2, n - 1)),
            dma((groups, 3)),
            dma((groups, 3)),
            dma((4, half)),
            dma((4, half)),
            dma((2,)),
        ],
        compiler_params=pltpu.CompilerParams(
            collective_id=0, has_side_effects=True, vmem_limit_bytes=56 * 1024 * 1024
        ),
        cost_estimate=pl.CostEstimate(
            flops=22 * 2 * count * height * 4 * height * width,
            bytes_accessed=2 * tiles.size * 2,
            transcendentals=0,
        ),
    )(tile_rows, keep.T, hand, slot, tiles)


def solution(mesh):
    placed = (P("col", None, "row", None), P("col", None), P("col", None), P("col"))
    return jax.shard_map(
        functools.partial(local, mesh.shape["col"]),
        mesh=mesh,
        in_specs=placed,
        out_specs=P("col", None, "row", None),
        check_vma=False,
    )
```

```python
import functools

import jax
import jax.numpy as jnp
from jax import lax
from jax.experimental import pallas as pl
from jax.experimental.pallas import tpu as pltpu
from jax.sharding import PartitionSpec as P

MESH = pl.DeviceIdType.MESH
NEAR = 4
STRIDE = 27
LEVELS = 32767.0


def coded(e):
    top = jnp.maximum(jnp.max(e, axis=0, keepdims=True), 1e-30)
    code = (e * (LEVELS / top) + 0.5).astype(jnp.int32).astype(jnp.int16)
    step = top * (1.0 / LEVELS)
    return code, step * step


def squared(code):
    value = code.astype(jnp.int32).astype(jnp.float32)
    return value * value


def kernel(
    n,
    rows_ref,
    keep_ref,
    hand_ref,
    slot_ref,
    source_ref,
    out_ref,
    tiles_ref,
    full,
    stage,
    arrived_a,
    arrived_b,
    acc,
    sums,
    sums_in,
    steps,
    factors,
    factors_in,
    early,
    early_in,
    late,
    late_in,
    x_send,
    x_recv,
    z_send,
    z_recv,
    s_send,
    s_recv,
    h_send,
    h_recv,
    own_sem,
):
    count, slots, height, width = tiles_ref.shape
    arrived = (arrived_a, arrived_b)
    half = count // 2
    part = height // 2
    me = lax.axis_index("col")
    x = lax.axis_index("row")
    up, down, across = lax.rem(x + 1, 4), lax.rem(x + 3, 4), lax.rem(x + 2, 4)
    partner = lax.rem(me + n // 2, n)
    mixed = (0,) + tuple(range(NEAR, slots))
    lag = 2
    ahead = 2
    pairs = count // 2
    groups = count // NEAR
    per = 2 * n // pairs

    held = pltpu.make_async_copy(source_ref, tiles_ref, own_sem.at[0])
    held.start()
    placed = pltpu.make_async_copy(source_ref, full.at[:, x], own_sem.at[1])
    placed.start()

    barrier = pltpu.get_barrier_semaphore()
    for peer in (up, down, across):
        pl.semaphore_signal(barrier, inc=1, device_id={"row": peer}, device_id_type=MESH)

    @pl.loop(1, n)
    def _(t):
        pl.semaphore_signal(
            barrier, inc=1, device_id={"col": lax.rem(me + t, n)}, device_id_type=MESH
        )

    sums[...] = jnp.zeros_like(sums)
    factors[...] = jnp.zeros_like(factors)
    held.wait()
    pl.semaphore_wait(barrier, n + 2)

    def direct(j, way):
        return pltpu.make_async_remote_copy(
            src_ref=tiles_ref.at[j],
            dst_ref=full.at[j, x],
            send_sem=x_send.at[way],
            recv_sem=x_recv.at[way, j],
            device_id={"row": (up, down)[way]},
            device_id_type=MESH,
        )

    def relay(j, way):
        origin = (down, up)[way]
        return pltpu.make_async_remote_copy(
            src_ref=full.at[j, origin],
            dst_ref=full.at[j, origin],
            send_sem=x_send.at[2],
            recv_sem=x_recv.at[2, j],
            device_id={"row": (up, down)[way]},
            device_id_type=MESH,
        )

    def far(h, t):
        return pltpu.make_async_remote_copy(
            src_ref=stage.at[h, t - 1],
            dst_ref=arrived[h].at[t - 1],
            send_sem=z_send.at[h],
            recv_sem=z_recv.at[h],
            device_id={"col": lax.rem(me + t, n)},
            device_id_type=MESH,
        )

    def all_far(h):
        return pltpu.make_async_remote_copy(
            src_ref=stage.at[h],
            dst_ref=arrived[h],
            send_sem=z_send.at[h],
            recv_sem=z_recv.at[h],
            device_id={"col": partner},
            device_id_type=MESH,
        )

    def all_rows(way):
        return pltpu.make_async_remote_copy(
            src_ref=tiles_ref,
            dst_ref=full.at[:, x],
            send_sem=x_send.at[way],
            recv_sem=x_recv.at[0, 0],
            device_id={"row": up},
            device_id_type=MESH,
        )

    def total(g, k):
        return pltpu.make_async_remote_copy(
            src_ref=sums.at[g],
            dst_ref=sums_in.at[k, g],
            send_sem=s_send.at[k],
            recv_sem=s_recv.at[g, k],
            device_id={"row": (up, down, across)[k]},
            device_id_type=MESH,
        )

    def to_partner(source, target, kind, i):
        return pltpu.make_async_remote_copy(
            src_ref=source,
            dst_ref=target,
            send_sem=h_send.at[kind],
            recv_sem=h_recv.at[kind, i],
            device_id={"col": partner},
            device_id_type=MESH,
        )

    def hand_late(h, j):
        return to_partner(late.at[h, j - half], late_in.at[h, j - half], h, j - half)

    def hand_early(j):
        return to_partner(early.at[j - half], early_in.at[j - half], 2, j - half)

    def hand_factor(j):
        return to_partner(factors.at[j - half], factors_in.at[j - half], 3, j - half)

    def send_far(number):
        i = lax.rem(number, n)
        t = lax.rem(i * STRIDE, n)
        pick = slot_ref[t]
        column = lax.rem(pick, count)
        for h in range(2):

            @pl.when((i > 0) & (number // n == h))
            def _():
                rows = pl.ds(h * part, part)
                stage[h, t - 1, 0] = tiles_ref[column, 0, rows]
                stage[h, t - 1, 1] = tiles_ref[column, NEAR + pick // count, rows]
                far(h, t).start()

    @pl.loop(0, lag)
    def _(p):
        for k in range(2):
            for way in range(2):
                direct(count - 1 - k - 2 * p, way).start()

                @pl.loop(0, per // 4)
                def _(m):
                    send_far(p * per + (2 * k + way) * (per // 4) + m)

    @pl.loop(lag * per, ahead * per)
    def _(number):
        send_far(number)

    placed.wait()

    def right(j, s):
        return full[j, :, s].reshape(4 * height, width)

    def row_of(ref, j):
        return ref[j // NEAR, pl.ds(lax.rem(j, NEAR), 1), :]

    def set_row(ref, j, value):
        ref[j // NEAR, pl.ds(lax.rem(j, NEAR), 1), :] = value

    def near(j, hands):
        left = []
        for s in range(NEAR):
            column = j if s == 0 else lax.rem(rows_ref[s, j], count)
            left.append(
                jnp.concatenate([tiles_ref[column, q ^ s] for q in range(NEAR)], axis=0)
            )
        a = jnp.concatenate(left, axis=1)
        b = jnp.concatenate([right(j, s) for s in range(NEAR)], axis=0)
        p = jnp.dot(a, b, preferred_element_type=jnp.float32).reshape(NEAR, height, width)
        acc[j, 0] = p[0]
        column_sum = jnp.zeros((1, width), jnp.float32)
        for q in range(1, NEAR):
            e = p[q] * keep_ref[q, j].astype(jnp.float32)
            if hands:
                early[j - half, q - 1], step = coded(e)
                steps[j - half, q - 1 : q, :] = step
            e = e * e
            acc[j, q] = e
            column_sum = column_sum + jnp.sum(e, axis=0, keepdims=True)
        set_row(sums, j, column_sum)
        c = tiles_ref[j, NEAR:].reshape((slots - NEAR) * height, width)
        acc[j, NEAR:] = jnp.dot(c, right(j, 0), preferred_element_type=jnp.float32).reshape(
            slots - NEAR, height, width
        )
        if hands:
            hand_early(j).start()

    def expand(h, columns, hands):
        rows = pl.ds(h * part, part)
        products = []
        for j in columns:
            for s in range(NEAR, slots):
                t = lax.rem(me - rows_ref[s, j] // count + n, n)
                a = arrived[h][jnp.maximum(t - 1, 0)].reshape(2 * part, width)
                products.append(
                    jnp.dot(a, right(j, s), preferred_element_type=jnp.float32)
                )
        for c, j in enumerate(columns):
            mine = products[c * (slots - NEAR) : (c + 1) * (slots - NEAR)]
            own = acc[j, 0, rows]
            for p in mine:
                own = own + p[part:]
            values = [own] + [acc[j, NEAR + i, rows] + p[:part] for i, p in enumerate(mine)]
            column_sum = row_of(sums, j)
            for i, q in enumerate(mixed):
                e = values[i] * keep_ref[q, j].astype(jnp.float32)
                if hands:
                    late[h, j - half, i], step = coded(e)
                    r = NEAR - 1 + h * len(mixed) + i
                    steps[j - half, r : r + 1, :] = step
                e = e * e
                acc[j, q, rows] = e
                column_sum = column_sum + jnp.sum(e, axis=0, keepdims=True)
            set_row(sums, j, column_sum)
            if hands:
                hand_late(h, j).start()

    def scale_of(j):
        whole = row_of(sums, j)
        for k in range(3):
            whole = whole + row_of(sums_in.at[k], j)
        return width / whole

    def pass_on(p):
        for k in range(2):
            j = count - 1 - k - 2 * p
            direct(j, k).wait_recv()
            relay(j, k).start()
            for way in range(2):

                @pl.when(p + lag < pairs)
                def _():
                    direct(j - 2 * lag, way).start()

                @pl.loop(0, per // 4)
                def _(m):
                    send_far((p + ahead) * per + (2 * k + way) * (per // 4) + m)

    def near_pair(p, hands):
        for k in range(2):
            j = count - 1 - k - 2 * p
            direct(j, 1 - k).wait_recv()
            relay(j, k).wait_recv()
            near(j, hands)

    def await_far(h):
        all_far(h).wait_recv()

    def expand_all(h, first, last, hands):
        @pl.loop(0, (last - first) // 2)
        def _(i):
            j = last - 1 - 2 * i
            expand(h, (j, j - 1), hands)

    def start_totals(g):
        for k in range(3):
            total(g, k).start()

    def await_totals(g):
        for k in range(3):
            total(g, k).wait_recv()

    def normalize(g):
        await_totals(g)

        @pl.loop(g * NEAR, (g + 1) * NEAR)
        def _(j):
            scale = scale_of(j)
            for q in range(slots):
                out_ref[j, q] = (acc[j, q] * scale).astype(jnp.bfloat16)

    @pl.loop(0, lag)
    def _(p):
        pass_on(p)

    @pl.loop(lag, pairs // 2 + lag)
    def _(p):
        pass_on(p)
        near_pair(p - lag, True)

    pass_on(pairs // 2 + lag)
    await_far(0)
    expand_all(0, half, count, True)
    near_pair(pairs // 2, False)
    pass_on(pairs // 2 + lag + 1)
    near_pair(pairs // 2 + 1, False)
    expand_all(0, NEAR, 2 * NEAR, False)

    await_far(1)
    for g in (3, 2, 1):
        expand_all(1, g * NEAR, (g + 1) * NEAR, g > 1)
        start_totals(g)

    for g in (3, 2):
        await_totals(g)

        @pl.loop(g * NEAR, (g + 1) * NEAR)
        def _(j):
            scale = scale_of(j)
            for r in range(NEAR - 1 + 2 * len(mixed)):
                factors[j - half, r : r + 1, :] = steps[j - half, r : r + 1, :] * scale
            hand_factor(j).start()

    @pl.loop(pairs // 2 + 2, pairs)
    def _(p):
        near_pair(p, False)

    expand_all(0, 0, NEAR, False)
    expand_all(1, 0, NEAR, False)
    start_totals(0)
    normalize(1)

    first = count - hand_ref[0]

    @pl.loop(0, half)
    def _(i):
        j = count - 1 - i
        hand_factor(j).wait_recv()
        hand_early(j).wait_recv()
        for h in range(2):
            hand_late(h, j).wait_recv()
        scale = scale_of(j)
        take = jnp.full((height, width), j, jnp.int32) >= first
        for q in range(1, NEAR):
            theirs = squared(early_in[j - half, q - 1]) * factors_in[j - half, q - 1 : q, :]
            out_ref[j, q] = jnp.where(take, theirs, acc[j, q] * scale).astype(jnp.bfloat16)
        for i, q in enumerate(mixed):
            for h in range(2):
                rows = pl.ds(h * part, part)
                r = NEAR - 1 + h * len(mixed) + i
                theirs = squared(late_in[h, j - half, i]) * factors_in[j - half, r : r + 1, :]
                out_ref[j, q, rows] = jnp.where(
                    take[:part], theirs, acc[j, q, rows] * scale
                ).astype(jnp.bfloat16)

    normalize(0)

    for way in range(3):
        all_rows(way).wait_send()
    for h in range(2):
        all_far(h).wait_send()
        to_partner(late.at[h], late_in.at[h], h, 0).wait_send()
    to_partner(early, early_in, 2, 0).wait_send()
    to_partner(factors, factors_in, 3, 0).wait_send()
    for k in range(3):
        pltpu.make_async_remote_copy(
            src_ref=sums,
            dst_ref=sums_in.at[k],
            send_sem=s_send.at[k],
            recv_sem=s_recv.at[0, k],
            device_id={"row": up},
            device_id_type=MESH,
        ).wait_send()


def local(n, tiles, tile_rows, keep, hand):
    count, slots, height, width = tiles.shape
    half = count // 2
    part = height // 2
    groups = count // NEAR
    far_count = slots - NEAR
    me = lax.axis_index("col")
    tile_rows = tile_rows.T
    owner = tile_rows[NEAR:] // count
    shift = (owner - me + n) % n
    request = jnp.arange(far_count * count, dtype=jnp.int32).reshape(far_count, count)
    turn = jnp.arange(n, dtype=jnp.int32)[:, None, None]
    slot = jnp.sum(jnp.where(shift[None] == turn, request[None], 0), (1, 2))
    smem = pl.BlockSpec(memory_space=pltpu.SMEM)
    vmem = pl.BlockSpec(memory_space=pltpu.VMEM)
    dma = pltpu.SemaphoreType.DMA
    return pl.pallas_call(
        functools.partial(kernel, n),
        out_shape=pltpu.VMEM(tiles.shape, tiles.dtype),
        in_specs=[smem, smem, smem, smem, pl.BlockSpec(memory_space=pl.ANY)],
        out_specs=vmem,
        scratch_shapes=[
            pltpu.VMEM(tiles.shape, tiles.dtype),
            pltpu.VMEM((count, 4, slots, height, width), jnp.bfloat16),
            pltpu.VMEM((2, n - 1, 2, part, width), jnp.bfloat16),
            pltpu.VMEM((n - 1, 2, part, width), jnp.bfloat16),
            pltpu.VMEM((n - 1, 2, part, width), jnp.bfloat16),
            pltpu.VMEM((count, slots, height, width), jnp.float32),
            pltpu.VMEM((groups, 8, width), jnp.float32),
            pltpu.VMEM((3, groups, 8, width), jnp.float32),
            pltpu.VMEM((half, 16, width), jnp.float32),
            pltpu.VMEM((half, 16, width), jnp.float32),
            pltpu.VMEM((half, 16, width), jnp.float32),
            pltpu.VMEM((half, NEAR - 1, height, width), jnp.int16),
            pltpu.VMEM((half, NEAR - 1, height, width), jnp.int16),
            pltpu.VMEM((2, half, 1 + far_count, part, width), jnp.int16),
            pltpu.VMEM((2, half, 1 + far_count, part, width), jnp.int16),
            dma((3,)),
            dma((3, count)),
            dma((2,)),
            dma((2,)),
            dma((3,)),
            dma((groups, 3)),
            dma((4,)),
            dma((4, half)),
            dma((2,)),
        ],
        compiler_params=pltpu.CompilerParams(
            collective_id=0, has_side_effects=True, vmem_limit_bytes=56 * 1024 * 1024
        ),
        cost_estimate=pl.CostEstimate(
            flops=22 * 2 * count * height * 4 * height * width,
            bytes_accessed=2 * tiles.size * 2,
            transcendentals=0,
        ),
    )(tile_rows, keep.T, hand, slot, tiles)


def solution(mesh):
    placed = (P("col", None, "row", None), P("col", None), P("col", None), P("col"))
    return jax.shard_map(
        functools.partial(local, mesh.shape["col"]),
        mesh=mesh,
        in_specs=placed,
        out_specs=P("col", None, "row", None),
        check_vma=False,
    )
```

```python
import functools

import jax
import jax.numpy as jnp
from jax import lax
from jax.experimental import pallas as pl
from jax.experimental.pallas import tpu as pltpu
from jax.sharding import PartitionSpec as P

MESH = pl.DeviceIdType.MESH
NEAR = 4
STRIDE = 27
LEVELS = 32767.0


def coded(e):
    top = jnp.maximum(jnp.max(e, axis=0, keepdims=True), 1e-30)
    code = (e * (LEVELS / top) + 0.5).astype(jnp.int32).astype(jnp.int16)
    step = top * (1.0 / LEVELS)
    return code, step * step


def squared(code):
    value = code.astype(jnp.int32).astype(jnp.float32)
    return value * value


def kernel(
    n,
    rows_ref,
    keep_ref,
    hand_ref,
    slot_ref,
    source_ref,
    out_ref,
    tiles_ref,
    full,
    stage,
    arrived_a,
    arrived_b,
    acc,
    sums,
    sums_in,
    steps,
    factors,
    factors_in,
    early,
    early_in,
    late,
    late_in,
    x_send,
    x_recv,
    z_send,
    z_recv,
    s_send,
    s_recv,
    h_send,
    h_recv,
    own_sem,
):
    count, slots, height, width = tiles_ref.shape
    arrived = (arrived_a, arrived_b)
    half = count // 2
    part = height // 2
    me = lax.axis_index("col")
    x = lax.axis_index("row")
    up, down, across = lax.rem(x + 1, 4), lax.rem(x + 3, 4), lax.rem(x + 2, 4)
    partner = lax.rem(me + n // 2, n)
    mixed = (0,) + tuple(range(NEAR, slots))
    lag = 2
    ahead = 2
    pairs = count // 2
    groups = count // NEAR
    per = 2 * n // pairs

    held = pltpu.make_async_copy(source_ref, tiles_ref, own_sem.at[0])
    held.start()
    placed = pltpu.make_async_copy(source_ref, full.at[:, x], own_sem.at[1])
    placed.start()

    barrier = pltpu.get_barrier_semaphore()
    for peer in (up, down, across):
        pl.semaphore_signal(barrier, inc=1, device_id={"row": peer}, device_id_type=MESH)

    @pl.loop(1, n)
    def _(t):
        pl.semaphore_signal(
            barrier, inc=1, device_id={"col": lax.rem(me + t, n)}, device_id_type=MESH
        )

    sums[...] = jnp.zeros_like(sums)
    factors[...] = jnp.zeros_like(factors)
    held.wait()
    pl.semaphore_wait(barrier, n + 2)

    def direct(j, way):
        return pltpu.make_async_remote_copy(
            src_ref=tiles_ref.at[j],
            dst_ref=full.at[j, x],
            send_sem=x_send.at[way],
            recv_sem=x_recv.at[way, j],
            device_id={"row": (up, down)[way]},
            device_id_type=MESH,
        )

    def relay(j, way):
        origin = (down, up)[way]
        return pltpu.make_async_remote_copy(
            src_ref=full.at[j, origin],
            dst_ref=full.at[j, origin],
            send_sem=x_send.at[2],
            recv_sem=x_recv.at[2, j],
            device_id={"row": (up, down)[way]},
            device_id_type=MESH,
        )

    def far(h, t):
        return pltpu.make_async_remote_copy(
            src_ref=stage.at[h, t - 1],
            dst_ref=arrived[h].at[t - 1],
            send_sem=z_send.at[h],
            recv_sem=z_recv.at[h],
            device_id={"col": lax.rem(me + t, n)},
            device_id_type=MESH,
        )

    def all_far(h):
        return pltpu.make_async_remote_copy(
            src_ref=stage.at[h],
            dst_ref=arrived[h],
            send_sem=z_send.at[h],
            recv_sem=z_recv.at[h],
            device_id={"col": partner},
            device_id_type=MESH,
        )

    def all_rows(way):
        return pltpu.make_async_remote_copy(
            src_ref=tiles_ref,
            dst_ref=full.at[:, x],
            send_sem=x_send.at[way],
            recv_sem=x_recv.at[0, 0],
            device_id={"row": up},
            device_id_type=MESH,
        )

    def total(g, k):
        return pltpu.make_async_remote_copy(
            src_ref=sums.at[g],
            dst_ref=sums_in.at[k, g],
            send_sem=s_send.at[k],
            recv_sem=s_recv.at[g, k],
            device_id={"row": (up, down, across)[k]},
            device_id_type=MESH,
        )

    def to_partner(source, target, kind, i):
        return pltpu.make_async_remote_copy(
            src_ref=source,
            dst_ref=target,
            send_sem=h_send.at[kind],
            recv_sem=h_recv.at[kind, i],
            device_id={"col": partner},
            device_id_type=MESH,
        )

    def hand_late(h, j):
        return to_partner(late.at[h, j - half], late_in.at[h, j - half], h, j - half)

    def hand_early(j):
        return to_partner(early.at[j - half], early_in.at[j - half], 2, j - half)

    def hand_factor(j):
        return to_partner(factors.at[j - half], factors_in.at[j - half], 3, j - half)

    def send_far(number):
        i = lax.rem(number, n)
        t = lax.rem(i * STRIDE, n)
        pick = slot_ref[t]
        column = lax.rem(pick, count)
        for h in range(2):

            @pl.when((i > 0) & (number // n == h))
            def _():
                rows = pl.ds(h * part, part)
                stage[h, t - 1, 0] = tiles_ref[column, 0, rows]
                stage[h, t - 1, 1] = tiles_ref[column, NEAR + pick // count, rows]
                far(h, t).start()

    @pl.loop(0, lag)
    def _(p):
        for k in range(2):
            for way in range(2):
                direct(count - 1 - k - 2 * p, way).start()

                @pl.loop(0, per // 4)
                def _(m):
                    send_far(p * per + (2 * k + way) * (per // 4) + m)

    @pl.loop(lag * per, ahead * per)
    def _(number):
        send_far(number)

    placed.wait()

    def right(j, s):
        return full[j, :, s].reshape(4 * height, width)

    def row_of(ref, j):
        return ref[j // NEAR, pl.ds(lax.rem(j, NEAR), 1), :]

    def set_row(ref, j, value):
        ref[j // NEAR, pl.ds(lax.rem(j, NEAR), 1), :] = value

    def near(j, hands):
        left = []
        for s in range(NEAR):
            column = j if s == 0 else lax.rem(rows_ref[s, j], count)
            left.append(
                jnp.concatenate([tiles_ref[column, q ^ s] for q in range(NEAR)], axis=0)
            )
        a = jnp.concatenate(left, axis=1)
        b = jnp.concatenate([right(j, s) for s in range(NEAR)], axis=0)
        p = jnp.dot(a, b, preferred_element_type=jnp.float32).reshape(NEAR, height, width)
        acc[j, 0] = p[0]
        column_sum = jnp.zeros((1, width), jnp.float32)
        for q in range(1, NEAR):
            e = p[q] * keep_ref[q, j].astype(jnp.float32)
            if hands:
                early[j - half, q - 1], step = coded(e)
                steps[j - half, q - 1 : q, :] = step
            e = e * e
            acc[j, q] = e
            column_sum = column_sum + jnp.sum(e, axis=0, keepdims=True)
        set_row(sums, j, column_sum)
        c = tiles_ref[j, NEAR:].reshape((slots - NEAR) * height, width)
        acc[j, NEAR:] = jnp.dot(c, right(j, 0), preferred_element_type=jnp.float32).reshape(
            slots - NEAR, height, width
        )
        if hands:
            hand_early(j).start()

    def expand(h, columns, hands):
        halves = (0, 1) if h is None else (h,)
        rows = pl.ds(halves[0] * part, len(halves) * part)
        products = []
        for j in columns:
            for s in range(NEAR, slots):
                t = lax.rem(me - rows_ref[s, j] // count + n, n)
                a = jnp.concatenate(
                    [arrived[i][jnp.maximum(t - 1, 0), k] for k in range(2) for i in halves], axis=0
                )
                products.append(jnp.dot(a, right(j, s), preferred_element_type=jnp.float32))
        edge = len(halves) * part
        for c, j in enumerate(columns):
            mine = products[c * (slots - NEAR) : (c + 1) * (slots - NEAR)]
            own = acc[j, 0, rows]
            for p in mine:
                own = own + p[edge:]
            values = [own] + [acc[j, NEAR + i, rows] + p[:edge] for i, p in enumerate(mine)]
            column_sum = row_of(sums, j)
            for i, q in enumerate(mixed):
                e = values[i] * keep_ref[q, j].astype(jnp.float32)
                if hands:
                    late[h, j - half, i], step = coded(e)
                    r = NEAR - 1 + h * len(mixed) + i
                    steps[j - half, r : r + 1, :] = step
                e = e * e
                acc[j, q, rows] = e
                column_sum = column_sum + jnp.sum(e, axis=0, keepdims=True)
            set_row(sums, j, column_sum)
            if hands:
                hand_late(h, j).start()

    def scale_of(j):
        whole = row_of(sums, j)
        for k in range(3):
            whole = whole + row_of(sums_in.at[k], j)
        return width / whole

    def pass_on(p):
        for k in range(2):
            j = count - 1 - k - 2 * p
            direct(j, k).wait_recv()
            relay(j, k).start()
            for way in range(2):

                @pl.when(p + lag < pairs)
                def _():
                    direct(j - 2 * lag, way).start()

                @pl.loop(0, per // 4)
                def _(m):
                    send_far((p + ahead) * per + (2 * k + way) * (per // 4) + m)

    def near_pair(p, hands):
        for k in range(2):
            j = count - 1 - k - 2 * p
            direct(j, 1 - k).wait_recv()
            relay(j, k).wait_recv()
            near(j, hands)

    def await_far(h):
        all_far(h).wait_recv()

    def expand_all(h, first, last, hands):
        @pl.loop(0, (last - first) // 2)
        def _(i):
            j = last - 1 - 2 * i
            expand(h, (j, j - 1), hands)

    def start_totals(g):
        for k in range(3):
            total(g, k).start()

    def await_totals(g):
        for k in range(3):
            total(g, k).wait_recv()

    def normalize(g):
        await_totals(g)

        @pl.loop(g * NEAR, (g + 1) * NEAR)
        def _(j):
            scale = scale_of(j)
            for q in range(slots):
                out_ref[j, q] = (acc[j, q] * scale).astype(jnp.bfloat16)

    @pl.loop(0, lag)
    def _(p):
        pass_on(p)

    @pl.loop(lag, pairs // 2 + lag)
    def _(p):
        pass_on(p)
        near_pair(p - lag, True)

    pass_on(pairs // 2 + lag)
    await_far(0)
    expand_all(0, half, count, True)
    near_pair(pairs // 2, False)
    pass_on(pairs // 2 + lag + 1)
    near_pair(pairs // 2 + 1, False)
    expand_all(0, NEAR, 2 * NEAR, False)

    await_far(1)
    for g in (3, 2, 1):
        expand_all(1, g * NEAR, (g + 1) * NEAR, g > 1)
        start_totals(g)

    for g in (3, 2):
        await_totals(g)

        @pl.loop(g * NEAR, (g + 1) * NEAR)
        def _(j):
            scale = scale_of(j)
            for r in range(NEAR - 1 + 2 * len(mixed)):
                factors[j - half, r : r + 1, :] = steps[j - half, r : r + 1, :] * scale
            hand_factor(j).start()

    near_pair(6, False)
    expand(None, (3, 2), False)
    normalize(1)
    near_pair(7, False)
    expand(None, (1, 0), False)
    start_totals(0)

    first = count - hand_ref[0]

    @pl.loop(0, half)
    def _(i):
        j = count - 1 - i
        hand_factor(j).wait_recv()
        hand_early(j).wait_recv()
        for h in range(2):
            hand_late(h, j).wait_recv()
        scale = scale_of(j)
        take = jnp.full((height, width), j, jnp.int32) >= first
        for q in range(1, NEAR):
            theirs = squared(early_in[j - half, q - 1]) * factors_in[j - half, q - 1 : q, :]
            out_ref[j, q] = jnp.where(take, theirs, acc[j, q] * scale).astype(jnp.bfloat16)
        for i, q in enumerate(mixed):
            for h in range(2):
                rows = pl.ds(h * part, part)
                r = NEAR - 1 + h * len(mixed) + i
                theirs = squared(late_in[h, j - half, i]) * factors_in[j - half, r : r + 1, :]
                out_ref[j, q, rows] = jnp.where(
                    take[:part], theirs, acc[j, q, rows] * scale
                ).astype(jnp.bfloat16)

    normalize(0)

    for way in range(3):
        all_rows(way).wait_send()
    for h in range(2):
        all_far(h).wait_send()
        to_partner(late.at[h], late_in.at[h], h, 0).wait_send()
    to_partner(early, early_in, 2, 0).wait_send()
    to_partner(factors, factors_in, 3, 0).wait_send()
    for k in range(3):
        pltpu.make_async_remote_copy(
            src_ref=sums,
            dst_ref=sums_in.at[k],
            send_sem=s_send.at[k],
            recv_sem=s_recv.at[0, k],
            device_id={"row": up},
            device_id_type=MESH,
        ).wait_send()


def local(n, tiles, tile_rows, keep, hand):
    count, slots, height, width = tiles.shape
    half = count // 2
    part = height // 2
    groups = count // NEAR
    far_count = slots - NEAR
    me = lax.axis_index("col")
    tile_rows = tile_rows.T
    owner = tile_rows[NEAR:] // count
    shift = (owner - me + n) % n
    request = jnp.arange(far_count * count, dtype=jnp.int32).reshape(far_count, count)
    turn = jnp.arange(n, dtype=jnp.int32)[:, None, None]
    slot = jnp.sum(jnp.where(shift[None] == turn, request[None], 0), (1, 2))
    smem = pl.BlockSpec(memory_space=pltpu.SMEM)
    vmem = pl.BlockSpec(memory_space=pltpu.VMEM)
    dma = pltpu.SemaphoreType.DMA
    return pl.pallas_call(
        functools.partial(kernel, n),
        out_shape=pltpu.VMEM(tiles.shape, tiles.dtype),
        in_specs=[smem, smem, smem, smem, pl.BlockSpec(memory_space=pl.ANY)],
        out_specs=vmem,
        scratch_shapes=[
            pltpu.VMEM(tiles.shape, tiles.dtype),
            pltpu.VMEM((count, 4, slots, height, width), jnp.bfloat16),
            pltpu.VMEM((2, n - 1, 2, part, width), jnp.bfloat16),
            pltpu.VMEM((n - 1, 2, part, width), jnp.bfloat16),
            pltpu.VMEM((n - 1, 2, part, width), jnp.bfloat16),
            pltpu.VMEM((count, slots, height, width), jnp.float32),
            pltpu.VMEM((groups, 8, width), jnp.float32),
            pltpu.VMEM((3, groups, 8, width), jnp.float32),
            pltpu.VMEM((half, 16, width), jnp.float32),
            pltpu.VMEM((half, 16, width), jnp.float32),
            pltpu.VMEM((half, 16, width), jnp.float32),
            pltpu.VMEM((half, NEAR - 1, height, width), jnp.int16),
            pltpu.VMEM((half, NEAR - 1, height, width), jnp.int16),
            pltpu.VMEM((2, half, 1 + far_count, part, width), jnp.int16),
            pltpu.VMEM((2, half, 1 + far_count, part, width), jnp.int16),
            dma((3,)),
            dma((3, count)),
            dma((2,)),
            dma((2,)),
            dma((3,)),
            dma((groups, 3)),
            dma((4,)),
            dma((4, half)),
            dma((2,)),
        ],
        compiler_params=pltpu.CompilerParams(
            collective_id=0, has_side_effects=True, vmem_limit_bytes=56 * 1024 * 1024
        ),
        cost_estimate=pl.CostEstimate(
            flops=22 * 2 * count * height * 4 * height * width,
            bytes_accessed=2 * tiles.size * 2,
            transcendentals=0,
        ),
    )(tile_rows, keep.T, hand, slot, tiles)


def solution(mesh):
    placed = (P("col", None, "row", None), P("col", None), P("col", None), P("col"))
    return jax.shard_map(
        functools.partial(local, mesh.shape["col"]),
        mesh=mesh,
        in_specs=placed,
        out_specs=P("col", None, "row", None),
        check_vma=False,
    )
```

```python
import functools

import jax
import jax.numpy as jnp
from jax import lax
from jax.experimental import pallas as pl
from jax.experimental.pallas import tpu as pltpu
from jax.sharding import PartitionSpec as P

MESH = pl.DeviceIdType.MESH
NEAR = 4
STRIDE = 27
LEVELS = 32767.0
LAST = 16


def coded(e):
    top = jnp.maximum(jnp.max(e, axis=0, keepdims=True), 1e-30)
    code = (e * (LEVELS / top) + 0.5).astype(jnp.int32).astype(jnp.int16)
    step = top * (1.0 / LEVELS)
    return code, step * step


def squared(code):
    value = code.astype(jnp.int32).astype(jnp.float32)
    return value * value


def kernel(
    n,
    rows_ref,
    keep_ref,
    hand_ref,
    slot_ref,
    source_ref,
    out_ref,
    tiles_ref,
    full,
    stage_a,
    stage_b,
    arrived_a,
    arrived_b,
    acc,
    sums,
    sums_in,
    steps,
    factors,
    factors_in,
    early,
    early_in,
    late_a,
    late_b,
    late_in_a,
    late_in_b,
    x_send,
    x_recv,
    z_send,
    z_recv,
    s_send,
    s_recv,
    h_send,
    h_recv,
    own_sem,
):
    count, slots, height, width = tiles_ref.shape
    stage, arrived = (stage_a, stage_b), (arrived_a, arrived_b)
    late, late_in = (late_a, late_b), (late_in_a, late_in_b)
    half = count // 2
    parts = ((0, height - LAST), (height - LAST, LAST))
    me = lax.axis_index("col")
    x = lax.axis_index("row")
    up, down, across = lax.rem(x + 1, 4), lax.rem(x + 3, 4), lax.rem(x + 2, 4)
    partner = lax.rem(me + n // 2, n)
    mixed = (0,) + tuple(range(NEAR, slots))
    lag = 2
    ahead = 2
    pairs = count // 2
    groups = count // NEAR
    per = 2 * n // pairs

    held = pltpu.make_async_copy(source_ref, tiles_ref, own_sem.at[0])
    held.start()
    placed = pltpu.make_async_copy(source_ref, full.at[:, x], own_sem.at[1])
    placed.start()

    barrier = pltpu.get_barrier_semaphore()
    for peer in (up, down, across):
        pl.semaphore_signal(barrier, inc=1, device_id={"row": peer}, device_id_type=MESH)

    @pl.loop(1, n)
    def _(t):
        pl.semaphore_signal(
            barrier, inc=1, device_id={"col": lax.rem(me + t, n)}, device_id_type=MESH
        )

    sums[...] = jnp.zeros_like(sums)
    factors[...] = jnp.zeros_like(factors)
    held.wait()
    pl.semaphore_wait(barrier, n + 2)

    def direct(j, way):
        return pltpu.make_async_remote_copy(
            src_ref=tiles_ref.at[j],
            dst_ref=full.at[j, x],
            send_sem=x_send.at[way],
            recv_sem=x_recv.at[way, j],
            device_id={"row": (up, down)[way]},
            device_id_type=MESH,
        )

    def relay(j, way):
        origin = (down, up)[way]
        return pltpu.make_async_remote_copy(
            src_ref=full.at[j, origin],
            dst_ref=full.at[j, origin],
            send_sem=x_send.at[2],
            recv_sem=x_recv.at[2, j],
            device_id={"row": (up, down)[way]},
            device_id_type=MESH,
        )

    def far(h, t):
        return pltpu.make_async_remote_copy(
            src_ref=stage[h].at[t - 1],
            dst_ref=arrived[h].at[t - 1],
            send_sem=z_send.at[h],
            recv_sem=z_recv.at[h],
            device_id={"col": lax.rem(me + t, n)},
            device_id_type=MESH,
        )

    def all_far(h):
        return pltpu.make_async_remote_copy(
            src_ref=stage[h],
            dst_ref=arrived[h],
            send_sem=z_send.at[h],
            recv_sem=z_recv.at[h],
            device_id={"col": partner},
            device_id_type=MESH,
        )

    def all_rows(way):
        return pltpu.make_async_remote_copy(
            src_ref=tiles_ref,
            dst_ref=full.at[:, x],
            send_sem=x_send.at[way],
            recv_sem=x_recv.at[0, 0],
            device_id={"row": up},
            device_id_type=MESH,
        )

    def total(g, k):
        return pltpu.make_async_remote_copy(
            src_ref=sums.at[g],
            dst_ref=sums_in.at[k, g],
            send_sem=s_send.at[k],
            recv_sem=s_recv.at[g, k],
            device_id={"row": (up, down, across)[k]},
            device_id_type=MESH,
        )

    def to_partner(source, target, kind, i):
        return pltpu.make_async_remote_copy(
            src_ref=source,
            dst_ref=target,
            send_sem=h_send.at[kind],
            recv_sem=h_recv.at[kind, i],
            device_id={"col": partner},
            device_id_type=MESH,
        )

    def hand_late(h, j):
        return to_partner(late[h].at[j - half], late_in[h].at[j - half], h, j - half)

    def hand_early(j):
        return to_partner(early.at[j - half], early_in.at[j - half], 2, j - half)

    def hand_factor(j):
        return to_partner(factors.at[j - half], factors_in.at[j - half], 3, j - half)

    def send_far(number):
        i = lax.rem(number, n)
        t = lax.rem(i * STRIDE, n)
        pick = slot_ref[t]
        column = lax.rem(pick, count)
        for h in range(2):

            @pl.when((i > 0) & (number // n == h))
            def _():
                rows = pl.ds(*parts[h])
                stage[h][t - 1, 0] = tiles_ref[column, 0, rows]
                stage[h][t - 1, 1] = tiles_ref[column, NEAR + pick // count, rows]
                far(h, t).start()

    @pl.loop(0, lag)
    def _(p):
        for k in range(2):
            for way in range(2):
                direct(count - 1 - k - 2 * p, way).start()

                @pl.loop(0, per // 4)
                def _(m):
                    send_far(p * per + (2 * k + way) * (per // 4) + m)

    @pl.loop(lag * per, ahead * per)
    def _(number):
        send_far(number)

    placed.wait()

    def right(j, s):
        return full[j, :, s].reshape(4 * height, width)

    def row_of(ref, j):
        return ref[j // NEAR, pl.ds(lax.rem(j, NEAR), 1), :]

    def set_row(ref, j, value):
        ref[j // NEAR, pl.ds(lax.rem(j, NEAR), 1), :] = value

    def near(j, hands):
        left = []
        for s in range(NEAR):
            column = j if s == 0 else lax.rem(rows_ref[s, j], count)
            left.append(
                jnp.concatenate([tiles_ref[column, q ^ s] for q in range(NEAR)], axis=0)
            )
        a = jnp.concatenate(left, axis=1)
        b = jnp.concatenate([right(j, s) for s in range(NEAR)], axis=0)
        p = jnp.dot(a, b, preferred_element_type=jnp.float32).reshape(NEAR, height, width)
        acc[j, 0] = p[0]
        column_sum = jnp.zeros((1, width), jnp.float32)
        for q in range(1, NEAR):
            e = p[q] * keep_ref[q, j].astype(jnp.float32)
            if hands:
                early[j - half, q - 1], step = coded(e)
                steps[j - half, q - 1 : q, :] = step
            e = e * e
            acc[j, q] = e
            column_sum = column_sum + jnp.sum(e, axis=0, keepdims=True)
        set_row(sums, j, column_sum)
        c = tiles_ref[j, NEAR:].reshape((slots - NEAR) * height, width)
        acc[j, NEAR:] = jnp.dot(c, right(j, 0), preferred_element_type=jnp.float32).reshape(
            slots - NEAR, height, width
        )
        if hands:
            hand_early(j).start()

    def expand(h, columns, hands):
        halves = (0, 1) if h is None else (h,)
        edge = sum(parts[i][1] for i in halves)
        rows = pl.ds(parts[halves[0]][0], edge)
        products = []
        for j in columns:
            for s in range(NEAR, slots):
                t = lax.rem(me - rows_ref[s, j] // count + n, n)
                a = jnp.concatenate(
                    [arrived[i][jnp.maximum(t - 1, 0), k] for k in range(2) for i in halves], axis=0
                )
                products.append(jnp.dot(a, right(j, s), preferred_element_type=jnp.float32))
        for c, j in enumerate(columns):
            mine = products[c * (slots - NEAR) : (c + 1) * (slots - NEAR)]
            own = acc[j, 0, rows]
            for p in mine:
                own = own + p[edge:]
            values = [own] + [acc[j, NEAR + i, rows] + p[:edge] for i, p in enumerate(mine)]
            column_sum = row_of(sums, j)
            for i, q in enumerate(mixed):
                e = values[i] * keep_ref[q, j].astype(jnp.float32)
                if hands:
                    late[h][j - half, i], step = coded(e)
                    r = NEAR - 1 + h * len(mixed) + i
                    steps[j - half, r : r + 1, :] = step
                e = e * e
                acc[j, q, rows] = e
                column_sum = column_sum + jnp.sum(e, axis=0, keepdims=True)
            set_row(sums, j, column_sum)
            if hands:
                hand_late(h, j).start()

    def scale_of(j):
        whole = row_of(sums, j)
        for k in range(3):
            whole = whole + row_of(sums_in.at[k], j)
        return width / whole

    def pass_on(p):
        for k in range(2):
            j = count - 1 - k - 2 * p
            direct(j, k).wait_recv()
            relay(j, k).start()
            for way in range(2):

                @pl.when(p + lag < pairs)
                def _():
                    direct(j - 2 * lag, way).start()

                @pl.loop(0, per // 4)
                def _(m):
                    send_far((p + ahead) * per + (2 * k + way) * (per // 4) + m)

    def near_pair(p, hands):
        for k in range(2):
            j = count - 1 - k - 2 * p
            direct(j, 1 - k).wait_recv()
            relay(j, k).wait_recv()
            near(j, hands)

    def await_far(h):
        all_far(h).wait_recv()

    def expand_all(h, first, last, hands):
        @pl.loop(0, (last - first) // 2)
        def _(i):
            j = last - 1 - 2 * i
            expand(h, (j, j - 1), hands)

    def start_totals(g):
        for k in range(3):
            total(g, k).start()

    def await_totals(g):
        for k in range(3):
            total(g, k).wait_recv()

    def normalize(g):
        await_totals(g)

        @pl.loop(g * NEAR, (g + 1) * NEAR)
        def _(j):
            scale = scale_of(j)
            for q in range(slots):
                out_ref[j, q] = (acc[j, q] * scale).astype(jnp.bfloat16)

    @pl.loop(0, lag)
    def _(p):
        pass_on(p)

    @pl.loop(lag, pairs // 2 + lag)
    def _(p):
        pass_on(p)
        near_pair(p - lag, True)

    pass_on(6)
    await_far(0)
    expand_all(0, half, count, True)
    near_pair(4, False)
    pass_on(7)
    await_far(1)
    for g in (3, 2):
        expand_all(1, g * NEAR, (g + 1) * NEAR, True)
        start_totals(g)
    near_pair(5, False)
    expand_all(None, NEAR, 2 * NEAR, False)
    start_totals(1)

    for g in (3, 2):
        await_totals(g)

        @pl.loop(g * NEAR, (g + 1) * NEAR)
        def _(j):
            scale = scale_of(j)
            for r in range(NEAR - 1 + 2 * len(mixed)):
                factors[j - half, r : r + 1, :] = steps[j - half, r : r + 1, :] * scale
            hand_factor(j).start()

    near_pair(6, False)
    expand(None, (3, 2), False)
    normalize(1)
    near_pair(7, False)
    expand(None, (1, 0), False)
    start_totals(0)

    first = count - hand_ref[0]

    @pl.loop(0, half)
    def _(i):
        j = count - 1 - i
        hand_factor(j).wait_recv()
        hand_early(j).wait_recv()
        for h in range(2):
            hand_late(h, j).wait_recv()
        scale = scale_of(j)
        take = jnp.full((height, width), j, jnp.int32) >= first
        for q in range(1, NEAR):
            theirs = squared(early_in[j - half, q - 1]) * factors_in[j - half, q - 1 : q, :]
            out_ref[j, q] = jnp.where(take, theirs, acc[j, q] * scale).astype(jnp.bfloat16)
        for i, q in enumerate(mixed):
            for h in range(2):
                rows = pl.ds(*parts[h])
                r = NEAR - 1 + h * len(mixed) + i
                theirs = squared(late_in[h][j - half, i]) * factors_in[j - half, r : r + 1, :]
                out_ref[j, q, rows] = jnp.where(
                    take[: parts[h][1]], theirs, acc[j, q, rows] * scale
                ).astype(jnp.bfloat16)

    normalize(0)

    for way in range(3):
        all_rows(way).wait_send()
    for h in range(2):
        all_far(h).wait_send()
        to_partner(late[h], late_in[h], h, 0).wait_send()
    to_partner(early, early_in, 2, 0).wait_send()
    to_partner(factors, factors_in, 3, 0).wait_send()
    for k in range(3):
        pltpu.make_async_remote_copy(
            src_ref=sums,
            dst_ref=sums_in.at[k],
            send_sem=s_send.at[k],
            recv_sem=s_recv.at[0, k],
            device_id={"row": up},
            device_id_type=MESH,
        ).wait_send()


def local(n, tiles, tile_rows, keep, hand):
    count, slots, height, width = tiles.shape
    half = count // 2
    groups = count // NEAR
    far_count = slots - NEAR
    me = lax.axis_index("col")
    tile_rows = tile_rows.T
    owner = tile_rows[NEAR:] // count
    shift = (owner - me + n) % n
    request = jnp.arange(far_count * count, dtype=jnp.int32).reshape(far_count, count)
    turn = jnp.arange(n, dtype=jnp.int32)[:, None, None]
    slot = jnp.sum(jnp.where(shift[None] == turn, request[None], 0), (1, 2))
    smem = pl.BlockSpec(memory_space=pltpu.SMEM)
    vmem = pl.BlockSpec(memory_space=pltpu.VMEM)
    dma = pltpu.SemaphoreType.DMA
    return pl.pallas_call(
        functools.partial(kernel, n),
        out_shape=pltpu.VMEM(tiles.shape, tiles.dtype),
        in_specs=[smem, smem, smem, smem, pl.BlockSpec(memory_space=pl.ANY)],
        out_specs=vmem,
        scratch_shapes=[
            pltpu.VMEM(tiles.shape, tiles.dtype),
            pltpu.VMEM((count, 4, slots, height, width), jnp.bfloat16),
            pltpu.VMEM((n - 1, 2, height - LAST, width), jnp.bfloat16),
            pltpu.VMEM((n - 1, 2, LAST, width), jnp.bfloat16),
            pltpu.VMEM((n - 1, 2, height - LAST, width), jnp.bfloat16),
            pltpu.VMEM((n - 1, 2, LAST, width), jnp.bfloat16),
            pltpu.VMEM((count, slots, height, width), jnp.float32),
            pltpu.VMEM((groups, 8, width), jnp.float32),
            pltpu.VMEM((3, groups, 8, width), jnp.float32),
            pltpu.VMEM((half, 16, width), jnp.float32),
            pltpu.VMEM((half, 16, width), jnp.float32),
            pltpu.VMEM((half, 16, width), jnp.float32),
            pltpu.VMEM((half, NEAR - 1, height, width), jnp.int16),
            pltpu.VMEM((half, NEAR - 1, height, width), jnp.int16),
            pltpu.VMEM((half, 1 + far_count, height - LAST, width), jnp.int16),
            pltpu.VMEM((half, 1 + far_count, LAST, width), jnp.int16),
            pltpu.VMEM((half, 1 + far_count, height - LAST, width), jnp.int16),
            pltpu.VMEM((half, 1 + far_count, LAST, width), jnp.int16),
            dma((3,)),
            dma((3, count)),
            dma((2,)),
            dma((2,)),
            dma((3,)),
            dma((groups, 3)),
            dma((4,)),
            dma((4, half)),
            dma((2,)),
        ],
        compiler_params=pltpu.CompilerParams(
            collective_id=0, has_side_effects=True, vmem_limit_bytes=56 * 1024 * 1024
        ),
        cost_estimate=pl.CostEstimate(
            flops=22 * 2 * count * height * 4 * height * width,
            bytes_accessed=2 * tiles.size * 2,
            transcendentals=0,
        ),
    )(tile_rows, keep.T, hand, slot, tiles)


def solution(mesh):
    placed = (P("col", None, "row", None), P("col", None), P("col", None), P("col"))
    return jax.shard_map(
        functools.partial(local, mesh.shape["col"]),
        mesh=mesh,
        in_specs=placed,
        out_specs=P("col", None, "row", None),
        check_vma=False,
    )
```

```python
import functools

import jax
import jax.numpy as jnp
from jax import lax
from jax.experimental import pallas as pl
from jax.experimental.pallas import tpu as pltpu
from jax.sharding import PartitionSpec as P

MESH = pl.DeviceIdType.MESH
NEAR = 4
STRIDE = 27
LEVELS = 32767.0
LAST = 16


def coded(e):
    top = jnp.maximum(jnp.max(e, axis=0, keepdims=True), 1e-30)
    code = (e * (LEVELS / top) + 0.5).astype(jnp.int32).astype(jnp.int16)
    step = top * (1.0 / LEVELS)
    return code, step * step


def squared(code):
    value = code.astype(jnp.int32).astype(jnp.float32)
    return value * value


def kernel(
    n,
    rows_ref,
    keep_ref,
    hand_ref,
    slot_ref,
    source_ref,
    out_ref,
    tiles_ref,
    full,
    stage_a,
    stage_b,
    arrived_a,
    arrived_b,
    acc,
    sums,
    sums_in,
    steps,
    factors,
    factors_in,
    early,
    early_in,
    late_a,
    late_b,
    late_in_a,
    late_in_b,
    x_send,
    x_recv,
    z_send,
    z_recv,
    s_send,
    s_recv,
    h_send,
    h_recv,
    own_sem,
):
    count, slots, height, width = tiles_ref.shape
    stage, arrived = (stage_a, stage_b), (arrived_a, arrived_b)
    late, late_in = (late_a, late_b), (late_in_a, late_in_b)
    half = count // 2
    parts = ((0, height - LAST), (height - LAST, LAST))
    me = lax.axis_index("col")
    x = lax.axis_index("row")
    up, down, across = lax.rem(x + 1, 4), lax.rem(x + 3, 4), lax.rem(x + 2, 4)
    partner = lax.rem(me + n // 2, n)
    mixed = (0,) + tuple(range(NEAR, slots))
    lag = 2
    ahead = 2
    pairs = count // 2
    groups = count // NEAR
    per = 2 * n // pairs

    held = pltpu.make_async_copy(source_ref, tiles_ref, own_sem.at[0])
    held.start()
    placed = pltpu.make_async_copy(source_ref, full.at[:, x], own_sem.at[1])
    placed.start()

    barrier = pltpu.get_barrier_semaphore()
    for peer in (up, down, across):
        pl.semaphore_signal(barrier, inc=1, device_id={"row": peer}, device_id_type=MESH)

    @pl.loop(1, n)
    def _(t):
        pl.semaphore_signal(
            barrier, inc=1, device_id={"col": lax.rem(me + t, n)}, device_id_type=MESH
        )

    sums[...] = jnp.zeros_like(sums)
    factors[...] = jnp.zeros_like(factors)
    held.wait()
    pl.semaphore_wait(barrier, n + 2)

    def direct(j, way):
        return pltpu.make_async_remote_copy(
            src_ref=tiles_ref.at[j],
            dst_ref=full.at[j, x],
            send_sem=x_send.at[way],
            recv_sem=x_recv.at[way, j],
            device_id={"row": (up, down)[way]},
            device_id_type=MESH,
        )

    def relay(j, way):
        origin = (down, up)[way]
        return pltpu.make_async_remote_copy(
            src_ref=full.at[j, origin],
            dst_ref=full.at[j, origin],
            send_sem=x_send.at[2],
            recv_sem=x_recv.at[2, j],
            device_id={"row": (up, down)[way]},
            device_id_type=MESH,
        )

    def far(h, t):
        return pltpu.make_async_remote_copy(
            src_ref=stage[h].at[t - 1],
            dst_ref=arrived[h].at[t - 1],
            send_sem=z_send.at[h],
            recv_sem=z_recv.at[h],
            device_id={"col": lax.rem(me + t, n)},
            device_id_type=MESH,
        )

    def all_far(h):
        return pltpu.make_async_remote_copy(
            src_ref=stage[h],
            dst_ref=arrived[h],
            send_sem=z_send.at[h],
            recv_sem=z_recv.at[h],
            device_id={"col": partner},
            device_id_type=MESH,
        )

    def all_rows(way):
        return pltpu.make_async_remote_copy(
            src_ref=tiles_ref,
            dst_ref=full.at[:, x],
            send_sem=x_send.at[way],
            recv_sem=x_recv.at[0, 0],
            device_id={"row": up},
            device_id_type=MESH,
        )

    def total(g, k):
        return pltpu.make_async_remote_copy(
            src_ref=sums.at[g],
            dst_ref=sums_in.at[k, g],
            send_sem=s_send.at[k],
            recv_sem=s_recv.at[g, k],
            device_id={"row": (up, down, across)[k]},
            device_id_type=MESH,
        )

    def to_partner(source, target, kind, i):
        return pltpu.make_async_remote_copy(
            src_ref=source,
            dst_ref=target,
            send_sem=h_send.at[kind],
            recv_sem=h_recv.at[kind, i],
            device_id={"col": partner},
            device_id_type=MESH,
        )

    def hand_late(h, j):
        return to_partner(late[h].at[j - half], late_in[h].at[j - half], h, j - half)

    def hand_early(j):
        return to_partner(early.at[j - half], early_in.at[j - half], 2, j - half)

    def hand_factor(j):
        return to_partner(factors.at[j - half], factors_in.at[j - half], 3, j - half)

    def send_far(number):
        i = lax.rem(number, n)
        t = lax.rem(i * STRIDE, n)
        pick = slot_ref[t]
        column = lax.rem(pick, count)
        for h in range(2):

            @pl.when((i > 0) & (number // n == h))
            def _():
                rows = pl.ds(*parts[h])
                stage[h][t - 1, 0] = tiles_ref[column, 0, rows]
                stage[h][t - 1, 1] = tiles_ref[column, NEAR + pick // count, rows]
                far(h, t).start()

    @pl.loop(0, lag)
    def _(p):
        for k in range(2):
            for way in range(2):
                direct(count - 1 - k - 2 * p, way).start()

                @pl.loop(0, per // 4)
                def _(m):
                    send_far(p * per + (2 * k + way) * (per // 4) + m)

    @pl.loop(lag * per, ahead * per)
    def _(number):
        send_far(number)

    placed.wait()

    def right(j, s):
        return full[j, :, s].reshape(4 * height, width)

    def row_of(ref, j):
        return ref[j // NEAR, pl.ds(lax.rem(j, NEAR), 1), :]

    def set_row(ref, j, value):
        ref[j // NEAR, pl.ds(lax.rem(j, NEAR), 1), :] = value

    def near(j, hands):
        left = []
        for s in range(NEAR):
            column = j if s == 0 else lax.rem(rows_ref[s, j], count)
            left.append(
                jnp.concatenate([tiles_ref[column, q ^ s] for q in range(NEAR)], axis=0)
            )
        a = jnp.concatenate(left, axis=1)
        b = jnp.concatenate([right(j, s) for s in range(NEAR)], axis=0)
        p = jnp.dot(a, b, preferred_element_type=jnp.float32).reshape(NEAR, height, width)
        acc[j, 0] = p[0]
        column_sum = jnp.zeros((1, width), jnp.float32)
        for q in range(1, NEAR):
            e = p[q] * keep_ref[q, j].astype(jnp.float32)
            if hands:
                early[j - half, q - 1], step = coded(e)
                steps[j - half, q - 1 : q, :] = step
            e = e * e
            acc[j, q] = e
            column_sum = column_sum + jnp.sum(e, axis=0, keepdims=True)
        set_row(sums, j, column_sum)
        c = tiles_ref[j, NEAR:].reshape((slots - NEAR) * height, width)
        acc[j, NEAR:] = jnp.dot(c, right(j, 0), preferred_element_type=jnp.float32).reshape(
            slots - NEAR, height, width
        )
        if hands:
            hand_early(j).start()

    def expand(h, columns, hands):
        halves = (0, 1) if h is None else (h,)
        edge = sum(parts[i][1] for i in halves)
        rows = pl.ds(parts[halves[0]][0], edge)
        products = []
        for j in columns:
            for s in range(NEAR, slots):
                t = lax.rem(me - rows_ref[s, j] // count + n, n)
                a = jnp.concatenate(
                    [arrived[i][jnp.maximum(t - 1, 0), k] for k in range(2) for i in halves], axis=0
                )
                products.append(jnp.dot(a, right(j, s), preferred_element_type=jnp.float32))
        for c, j in enumerate(columns):
            mine = products[c * (slots - NEAR) : (c + 1) * (slots - NEAR)]
            own = acc[j, 0, rows]
            for p in mine:
                own = own + p[edge:]
            values = [own] + [acc[j, NEAR + i, rows] + p[:edge] for i, p in enumerate(mine)]
            column_sum = row_of(sums, j)
            for i, q in enumerate(mixed):
                e = values[i] * keep_ref[q, j].astype(jnp.float32)
                if hands:
                    late[h][j - half, i], step = coded(e)
                    r = NEAR - 1 + h * len(mixed) + i
                    steps[j - half, r : r + 1, :] = step
                e = e * e
                acc[j, q, rows] = e
                column_sum = column_sum + jnp.sum(e, axis=0, keepdims=True)
            set_row(sums, j, column_sum)
            if hands:
                hand_late(h, j).start()

    def scale_of(j):
        whole = row_of(sums, j)
        for k in range(3):
            whole = whole + row_of(sums_in.at[k], j)
        return width / whole

    def pass_on(p):
        for k in range(2):
            j = count - 1 - k - 2 * p
            direct(j, k).wait_recv()
            relay(j, k).start()
            for way in range(2):

                @pl.when(p + lag < pairs)
                def _():
                    direct(j - 2 * lag, way).start()

                @pl.loop(0, per // 4)
                def _(m):
                    send_far((p + ahead) * per + (2 * k + way) * (per // 4) + m)

    def near_pair(p, hands):
        for k in range(2):
            j = count - 1 - k - 2 * p
            direct(j, 1 - k).wait_recv()
            relay(j, k).wait_recv()
            near(j, hands)

    def await_far(h):
        all_far(h).wait_recv()

    def expand_all(h, first, last, hands):
        @pl.loop(0, (last - first) // 2)
        def _(i):
            j = last - 1 - 2 * i
            expand(h, (j, j - 1), hands)

    def start_totals(g):
        for k in range(3):
            total(g, k).start()

    def await_totals(g):
        for k in range(3):
            total(g, k).wait_recv()

    def normalize(g):
        await_totals(g)

        @pl.loop(g * NEAR, (g + 1) * NEAR)
        def _(j):
            scale = scale_of(j)
            for q in range(slots):
                out_ref[j, q] = (acc[j, q] * scale).astype(jnp.bfloat16)

    @pl.loop(0, lag)
    def _(p):
        pass_on(p)

    @pl.loop(lag, pairs // 2 + lag)
    def _(p):
        pass_on(p)
        near_pair(p - lag, True)

    pass_on(6)
    await_far(0)
    expand_all(0, half, count, True)
    near_pair(4, False)
    pass_on(7)
    await_far(1)
    for g in (3, 2):
        expand_all(1, g * NEAR, (g + 1) * NEAR, True)
        start_totals(g)
    near_pair(5, False)
    expand_all(None, NEAR, 2 * NEAR, False)
    start_totals(1)

    for g in (3, 2):
        await_totals(g)

        @pl.loop(g * NEAR, (g + 1) * NEAR)
        def _(j):
            scale = scale_of(j)
            for r in range(NEAR - 1 + 2 * len(mixed)):
                factors[j - half, r : r + 1, :] = steps[j - half, r : r + 1, :] * scale
            hand_factor(j).start()

    first = count - hand_ref[0]

    def finish(g):
        @pl.loop(0, NEAR)
        def _(i):
            j = (g + 1) * NEAR - 1 - i
            hand_factor(j).wait_recv()
            hand_early(j).wait_recv()
            for h in range(2):
                hand_late(h, j).wait_recv()
            scale = scale_of(j)
            take = jnp.full((height, width), j, jnp.int32) >= first
            for q in range(1, NEAR):
                theirs = squared(early_in[j - half, q - 1]) * factors_in[j - half, q - 1 : q, :]
                out_ref[j, q] = jnp.where(take, theirs, acc[j, q] * scale).astype(jnp.bfloat16)
            for i, q in enumerate(mixed):
                for h in range(2):
                    rows = pl.ds(*parts[h])
                    r = NEAR - 1 + h * len(mixed) + i
                    theirs = squared(late_in[h][j - half, i]) * factors_in[j - half, r : r + 1, :]
                    out_ref[j, q, rows] = jnp.where(
                        take[: parts[h][1]], theirs, acc[j, q, rows] * scale
                    ).astype(jnp.bfloat16)


    near_pair(6, False)
    expand(None, (3, 2), False)
    normalize(1)
    finish(3)
    near_pair(7, False)
    expand(None, (1, 0), False)
    start_totals(0)
    finish(2)
    normalize(0)

    for way in range(3):
        all_rows(way).wait_send()
    for h in range(2):
        all_far(h).wait_send()
        to_partner(late[h], late_in[h], h, 0).wait_send()
    to_partner(early, early_in, 2, 0).wait_send()
    to_partner(factors, factors_in, 3, 0).wait_send()
    for k in range(3):
        pltpu.make_async_remote_copy(
            src_ref=sums,
            dst_ref=sums_in.at[k],
            send_sem=s_send.at[k],
            recv_sem=s_recv.at[0, k],
            device_id={"row": up},
            device_id_type=MESH,
        ).wait_send()


def local(n, tiles, tile_rows, keep, hand):
    count, slots, height, width = tiles.shape
    half = count // 2
    groups = count // NEAR
    far_count = slots - NEAR
    me = lax.axis_index("col")
    tile_rows = tile_rows.T
    shape = (n, far_count, count)
    low = lax.broadcasted_iota(jnp.int32, shape, 0) * count
    request = lax.broadcasted_iota(jnp.int32, shape, 1) * count + lax.broadcasted_iota(
        jnp.int32, shape, 2
    )
    ahead = tile_rows[NEAR:] - me * count
    ahead = jnp.broadcast_to(jnp.where(ahead < 0, ahead + n * count, ahead)[None], shape)
    slot = jnp.sum(jnp.where((ahead >= low) & (ahead < low + count), request, 0), (1, 2))
    smem = pl.BlockSpec(memory_space=pltpu.SMEM)
    vmem = pl.BlockSpec(memory_space=pltpu.VMEM)
    dma = pltpu.SemaphoreType.DMA
    return pl.pallas_call(
        functools.partial(kernel, n),
        out_shape=pltpu.VMEM(tiles.shape, tiles.dtype),
        in_specs=[smem, smem, smem, smem, pl.BlockSpec(memory_space=pl.ANY)],
        out_specs=vmem,
        scratch_shapes=[
            pltpu.VMEM(tiles.shape, tiles.dtype),
            pltpu.VMEM((count, 4, slots, height, width), jnp.bfloat16),
            pltpu.VMEM((n - 1, 2, height - LAST, width), jnp.bfloat16),
            pltpu.VMEM((n - 1, 2, LAST, width), jnp.bfloat16),
            pltpu.VMEM((n - 1, 2, height - LAST, width), jnp.bfloat16),
            pltpu.VMEM((n - 1, 2, LAST, width), jnp.bfloat16),
            pltpu.VMEM((count, slots, height, width), jnp.float32),
            pltpu.VMEM((groups, 8, width), jnp.float32),
            pltpu.VMEM((3, groups, 8, width), jnp.float32),
            pltpu.VMEM((half, 16, width), jnp.float32),
            pltpu.VMEM((half, 16, width), jnp.float32),
            pltpu.VMEM((half, 16, width), jnp.float32),
            pltpu.VMEM((half, NEAR - 1, height, width), jnp.int16),
            pltpu.VMEM((half, NEAR - 1, height, width), jnp.int16),
            pltpu.VMEM((half, 1 + far_count, height - LAST, width), jnp.int16),
            pltpu.VMEM((half, 1 + far_count, LAST, width), jnp.int16),
            pltpu.VMEM((half, 1 + far_count, height - LAST, width), jnp.int16),
            pltpu.VMEM((half, 1 + far_count, LAST, width), jnp.int16),
            dma((3,)),
            dma((3, count)),
            dma((2,)),
            dma((2,)),
            dma((3,)),
            dma((groups, 3)),
            dma((4,)),
            dma((4, half)),
            dma((2,)),
        ],
        compiler_params=pltpu.CompilerParams(
            collective_id=0, has_side_effects=True, vmem_limit_bytes=56 * 1024 * 1024
        ),
        cost_estimate=pl.CostEstimate(
            flops=22 * 2 * count * height * 4 * height * width,
            bytes_accessed=2 * tiles.size * 2,
            transcendentals=0,
        ),
    )(tile_rows, keep.T, hand, slot, tiles)


def solution(mesh):
    placed = (P("col", None, "row", None), P("col", None), P("col", None), P("col"))
    return jax.shard_map(
        functools.partial(local, mesh.shape["col"]),
        mesh=mesh,
        in_specs=placed,
        out_specs=P("col", None, "row", None),
        check_vma=False,
    )
```

```python
import functools

import jax
import jax.numpy as jnp
from jax import lax
from jax.experimental import pallas as pl
from jax.experimental.pallas import tpu as pltpu
from jax.sharding import PartitionSpec as P

MESH = pl.DeviceIdType.MESH
NEAR = 4
STRIDE = 27
LEVELS = 32767.0
LAST = 16


def coded(e):
    top = jnp.maximum(jnp.max(e, axis=0, keepdims=True), 1e-30)
    code = (e * (LEVELS / top) + 0.5).astype(jnp.int32).astype(jnp.int16)
    step = top * (1.0 / LEVELS)
    return code, step * step


def squared(code):
    value = code.astype(jnp.int32).astype(jnp.float32)
    return value * value


def kernel(
    n,
    rows_ref,
    keep_ref,
    hand_ref,
    slot_ref,
    source_ref,
    out_ref,
    tiles_ref,
    full,
    stage_a,
    stage_b,
    arrived_a,
    arrived_b,
    acc,
    sums,
    sums_in,
    steps,
    factors,
    factors_in,
    early,
    early_in,
    late_a,
    late_b,
    late_in_a,
    late_in_b,
    x_send,
    x_recv,
    z_send,
    z_recv,
    s_send,
    s_recv,
    h_send,
    h_recv,
    own_sem,
):
    count, slots, height, width = tiles_ref.shape
    stage, arrived = (stage_a, stage_b), (arrived_a, arrived_b)
    late, late_in = (late_a, late_b), (late_in_a, late_in_b)
    half = count // 2
    parts = ((0, height - LAST), (height - LAST, LAST))
    me = lax.axis_index("col")
    x = lax.axis_index("row")
    up, down, across = lax.rem(x + 1, 4), lax.rem(x + 3, 4), lax.rem(x + 2, 4)
    partner = lax.rem(me + n // 2, n)
    mixed = (0,) + tuple(range(NEAR, slots))
    lag = 2
    ahead = 4
    pairs = count // 2
    groups = count // NEAR
    per = 2 * n // pairs

    held = pltpu.make_async_copy(source_ref, tiles_ref, own_sem.at[0])
    held.start()
    placed = pltpu.make_async_copy(source_ref, full.at[:, x], own_sem.at[1])
    placed.start()

    barrier = pltpu.get_barrier_semaphore()
    for peer in (up, down, across):
        pl.semaphore_signal(barrier, inc=1, device_id={"row": peer}, device_id_type=MESH)

    @pl.loop(1, n)
    def _(t):
        pl.semaphore_signal(
            barrier, inc=1, device_id={"col": lax.rem(me + t, n)}, device_id_type=MESH
        )

    sums[...] = jnp.zeros_like(sums)
    factors[...] = jnp.zeros_like(factors)
    held.wait()
    pl.semaphore_wait(barrier, n + 2)

    def direct(j, way):
        return pltpu.make_async_remote_copy(
            src_ref=tiles_ref.at[j],
            dst_ref=full.at[j, x],
            send_sem=x_send.at[way],
            recv_sem=x_recv.at[way, j],
            device_id={"row": (up, down)[way]},
            device_id_type=MESH,
        )

    def relay(j, way):
        origin = (down, up)[way]
        return pltpu.make_async_remote_copy(
            src_ref=full.at[j, origin],
            dst_ref=full.at[j, origin],
            send_sem=x_send.at[2],
            recv_sem=x_recv.at[2, j],
            device_id={"row": (up, down)[way]},
            device_id_type=MESH,
        )

    def far(h, t):
        return pltpu.make_async_remote_copy(
            src_ref=stage[h].at[t - 1],
            dst_ref=arrived[h].at[t - 1],
            send_sem=z_send.at[h],
            recv_sem=z_recv.at[h],
            device_id={"col": lax.rem(me + t, n)},
            device_id_type=MESH,
        )

    def all_far(h):
        return pltpu.make_async_remote_copy(
            src_ref=stage[h],
            dst_ref=arrived[h],
            send_sem=z_send.at[h],
            recv_sem=z_recv.at[h],
            device_id={"col": partner},
            device_id_type=MESH,
        )

    def all_rows(way):
        return pltpu.make_async_remote_copy(
            src_ref=tiles_ref,
            dst_ref=full.at[:, x],
            send_sem=x_send.at[way],
            recv_sem=x_recv.at[0, 0],
            device_id={"row": up},
            device_id_type=MESH,
        )

    def total(g, k):
        return pltpu.make_async_remote_copy(
            src_ref=sums.at[g],
            dst_ref=sums_in.at[k, g],
            send_sem=s_send.at[k],
            recv_sem=s_recv.at[g, k],
            device_id={"row": (up, down, across)[k]},
            device_id_type=MESH,
        )

    def to_partner(source, target, kind, i):
        return pltpu.make_async_remote_copy(
            src_ref=source,
            dst_ref=target,
            send_sem=h_send.at[kind],
            recv_sem=h_recv.at[kind, i],
            device_id={"col": partner},
            device_id_type=MESH,
        )

    def hand_late(h, j):
        return to_partner(late[h].at[j - half], late_in[h].at[j - half], h, j - half)

    def hand_early(j):
        return to_partner(early.at[j - half], early_in.at[j - half], 2, j - half)

    def hand_factor(j):
        return to_partner(factors.at[j - half], factors_in.at[j - half], 3, j - half)

    def send_far(number):
        i = lax.rem(number, n)
        t = lax.rem(i * STRIDE, n)
        pick = slot_ref[t]
        column = lax.rem(pick, count)
        for h in range(2):

            @pl.when((i > 0) & (number // n == h))
            def _():
                rows = pl.ds(*parts[h])
                stage[h][t - 1, 0] = tiles_ref[column, 0, rows]
                stage[h][t - 1, 1] = tiles_ref[column, NEAR + pick // count, rows]
                far(h, t).start()

    @pl.loop(0, lag)
    def _(p):
        for k in range(2):
            for way in range(2):
                direct(count - 1 - k - 2 * p, way).start()

                @pl.loop(0, per // 4)
                def _(m):
                    send_far(p * per + (2 * k + way) * (per // 4) + m)

    @pl.loop(lag * per, ahead * per)
    def _(number):
        send_far(number)

    placed.wait()

    def right(j, s):
        return full[j, :, s].reshape(4 * height, width)

    def row_of(ref, j):
        return ref[j // NEAR, pl.ds(lax.rem(j, NEAR), 1), :]

    def set_row(ref, j, value):
        ref[j // NEAR, pl.ds(lax.rem(j, NEAR), 1), :] = value

    def near(j, hands):
        left = []
        for s in range(NEAR):
            column = j if s == 0 else lax.rem(rows_ref[s, j], count)
            left.append(
                jnp.concatenate([tiles_ref[column, q ^ s] for q in range(NEAR)], axis=0)
            )
        a = jnp.concatenate(left, axis=1)
        b = jnp.concatenate([right(j, s) for s in range(NEAR)], axis=0)
        p = jnp.dot(a, b, preferred_element_type=jnp.float32).reshape(NEAR, height, width)
        acc[j, 0] = p[0]
        column_sum = jnp.zeros((1, width), jnp.float32)
        for q in range(1, NEAR):
            e = p[q] * keep_ref[q, j].astype(jnp.float32)
            if hands:
                early[j - half, q - 1], step = coded(e)
                steps[j - half, q - 1 : q, :] = step
            e = e * e
            acc[j, q] = e
            column_sum = column_sum + jnp.sum(e, axis=0, keepdims=True)
        set_row(sums, j, column_sum)
        c = tiles_ref[j, NEAR:].reshape((slots - NEAR) * height, width)
        acc[j, NEAR:] = jnp.dot(c, right(j, 0), preferred_element_type=jnp.float32).reshape(
            slots - NEAR, height, width
        )
        if hands:
            hand_early(j).start()

    def expand(h, columns, hands):
        halves = (0, 1) if h is None else (h,)
        edge = sum(parts[i][1] for i in halves)
        rows = pl.ds(parts[halves[0]][0], edge)
        products = []
        for j in columns:
            for s in range(NEAR, slots):
                t = lax.rem(me - rows_ref[s, j] // count + n, n)
                a = jnp.concatenate(
                    [arrived[i][jnp.maximum(t - 1, 0), k] for k in range(2) for i in halves], axis=0
                )
                products.append(jnp.dot(a, right(j, s), preferred_element_type=jnp.float32))
        for c, j in enumerate(columns):
            mine = products[c * (slots - NEAR) : (c + 1) * (slots - NEAR)]
            own = acc[j, 0, rows]
            for p in mine:
                own = own + p[edge:]
            values = [own] + [acc[j, NEAR + i, rows] + p[:edge] for i, p in enumerate(mine)]
            column_sum = row_of(sums, j)
            for i, q in enumerate(mixed):
                e = values[i] * keep_ref[q, j].astype(jnp.float32)
                if hands:
                    late[h][j - half, i], step = coded(e)
                    r = NEAR - 1 + h * len(mixed) + i
                    steps[j - half, r : r + 1, :] = step
                e = e * e
                acc[j, q, rows] = e
                column_sum = column_sum + jnp.sum(e, axis=0, keepdims=True)
            set_row(sums, j, column_sum)
            if hands:
                hand_late(h, j).start()

    def scale_of(j):
        whole = row_of(sums, j)
        for k in range(3):
            whole = whole + row_of(sums_in.at[k], j)
        return width / whole

    def pass_on(p):
        for k in range(2):
            j = count - 1 - k - 2 * p
            direct(j, k).wait_recv()
            relay(j, k).start()
            for way in range(2):

                @pl.when(p + lag < pairs)
                def _():
                    direct(j - 2 * lag, way).start()

                @pl.loop(0, per // 4)
                def _(m):
                    send_far((p + ahead) * per + (2 * k + way) * (per // 4) + m)

    def near_pair(p, hands):
        for k in range(2):
            j = count - 1 - k - 2 * p
            direct(j, 1 - k).wait_recv()
            relay(j, k).wait_recv()
            near(j, hands)

    def await_far(h):
        all_far(h).wait_recv()

    def expand_all(h, first, last, hands):
        @pl.loop(0, (last - first) // 2)
        def _(i):
            j = last - 1 - 2 * i
            expand(h, (j, j - 1), hands)

    def start_totals(g):
        for k in range(3):
            total(g, k).start()

    def await_totals(g):
        for k in range(3):
            total(g, k).wait_recv()

    def normalize(g):
        await_totals(g)

        @pl.loop(g * NEAR, (g + 1) * NEAR)
        def _(j):
            scale = scale_of(j)
            for q in range(slots):
                out_ref[j, q] = (acc[j, q] * scale).astype(jnp.bfloat16)

    @pl.loop(0, lag)
    def _(p):
        pass_on(p)

    @pl.loop(lag, pairs // 2 + lag)
    def _(p):
        pass_on(p)
        near_pair(p - lag, True)

    pass_on(6)
    await_far(0)
    expand_all(0, half, count, True)
    near_pair(4, False)
    pass_on(7)
    await_far(1)
    for g in (3, 2):
        expand_all(1, g * NEAR, (g + 1) * NEAR, True)
        start_totals(g)

    for g in (3, 2):
        await_totals(g)

        @pl.loop(g * NEAR, (g + 1) * NEAR)
        def _(j):
            scale = scale_of(j)
            for r in range(NEAR - 1 + 2 * len(mixed)):
                factors[j - half, r : r + 1, :] = steps[j - half, r : r + 1, :] * scale
            hand_factor(j).start()

    near_pair(5, False)
    expand_all(None, NEAR, 2 * NEAR, False)
    start_totals(1)

    near_pair(6, False)
    expand(None, (3, 2), False)
    normalize(1)
    near_pair(7, False)
    expand(None, (1, 0), False)
    start_totals(0)

    first = count - hand_ref[0]

    @pl.loop(0, half)
    def _(i):
        j = count - 1 - i
        hand_factor(j).wait_recv()
        hand_early(j).wait_recv()
        for h in range(2):
            hand_late(h, j).wait_recv()
        scale = scale_of(j)
        take = jnp.full((height, width), j, jnp.int32) >= first
        for q in range(1, NEAR):
            theirs = squared(early_in[j - half, q - 1]) * factors_in[j - half, q - 1 : q, :]
            out_ref[j, q] = jnp.where(take, theirs, acc[j, q] * scale).astype(jnp.bfloat16)
        for i, q in enumerate(mixed):
            for h in range(2):
                rows = pl.ds(*parts[h])
                r = NEAR - 1 + h * len(mixed) + i
                theirs = squared(late_in[h][j - half, i]) * factors_in[j - half, r : r + 1, :]
                out_ref[j, q, rows] = jnp.where(
                    take[: parts[h][1]], theirs, acc[j, q, rows] * scale
                ).astype(jnp.bfloat16)

    normalize(0)

    for way in range(3):
        all_rows(way).wait_send()
    for h in range(2):
        all_far(h).wait_send()
        to_partner(late[h], late_in[h], h, 0).wait_send()
    to_partner(early, early_in, 2, 0).wait_send()
    to_partner(factors, factors_in, 3, 0).wait_send()
    for k in range(3):
        pltpu.make_async_remote_copy(
            src_ref=sums,
            dst_ref=sums_in.at[k],
            send_sem=s_send.at[k],
            recv_sem=s_recv.at[0, k],
            device_id={"row": up},
            device_id_type=MESH,
        ).wait_send()


def local(n, tiles, tile_rows, keep, hand):
    count, slots, height, width = tiles.shape
    half = count // 2
    groups = count // NEAR
    far_count = slots - NEAR
    me = lax.axis_index("col")
    tile_rows = tile_rows.T
    owner = tile_rows[NEAR:] // count
    shift = (owner - me + n) % n
    request = jnp.arange(far_count * count, dtype=jnp.int32).reshape(far_count, count)
    turn = jnp.arange(n, dtype=jnp.int32)[:, None, None]
    slot = jnp.sum(jnp.where(shift[None] == turn, request[None], 0), (1, 2))
    smem = pl.BlockSpec(memory_space=pltpu.SMEM)
    vmem = pl.BlockSpec(memory_space=pltpu.VMEM)
    dma = pltpu.SemaphoreType.DMA
    return pl.pallas_call(
        functools.partial(kernel, n),
        out_shape=pltpu.VMEM(tiles.shape, tiles.dtype),
        in_specs=[smem, smem, smem, smem, pl.BlockSpec(memory_space=pl.ANY)],
        out_specs=vmem,
        scratch_shapes=[
            pltpu.VMEM(tiles.shape, tiles.dtype),
            pltpu.VMEM((count, 4, slots, height, width), jnp.bfloat16),
            pltpu.VMEM((n - 1, 2, height - LAST, width), jnp.bfloat16),
            pltpu.VMEM((n - 1, 2, LAST, width), jnp.bfloat16),
            pltpu.VMEM((n - 1, 2, height - LAST, width), jnp.bfloat16),
            pltpu.VMEM((n - 1, 2, LAST, width), jnp.bfloat16),
            pltpu.VMEM((count, slots, height, width), jnp.float32),
            pltpu.VMEM((groups, 8, width), jnp.float32),
            pltpu.VMEM((3, groups, 8, width), jnp.float32),
            pltpu.VMEM((half, 16, width), jnp.float32),
            pltpu.VMEM((half, 16, width), jnp.float32),
            pltpu.VMEM((half, 16, width), jnp.float32),
            pltpu.VMEM((half, NEAR - 1, height, width), jnp.int16),
            pltpu.VMEM((half, NEAR - 1, height, width), jnp.int16),
            pltpu.VMEM((half, 1 + far_count, height - LAST, width), jnp.int16),
            pltpu.VMEM((half, 1 + far_count, LAST, width), jnp.int16),
            pltpu.VMEM((half, 1 + far_count, height - LAST, width), jnp.int16),
            pltpu.VMEM((half, 1 + far_count, LAST, width), jnp.int16),
            dma((3,)),
            dma((3, count)),
            dma((2,)),
            dma((2,)),
            dma((3,)),
            dma((groups, 3)),
            dma((4,)),
            dma((4, half)),
            dma((2,)),
        ],
        compiler_params=pltpu.CompilerParams(
            collective_id=0, has_side_effects=True, vmem_limit_bytes=56 * 1024 * 1024
        ),
        cost_estimate=pl.CostEstimate(
            flops=22 * 2 * count * height * 4 * height * width,
            bytes_accessed=2 * tiles.size * 2,
            transcendentals=0,
        ),
    )(tile_rows, keep.T, hand, slot, tiles)


def solution(mesh):
    placed = (P("col", None, "row", None), P("col", None), P("col", None), P("col"))
    return jax.shard_map(
        functools.partial(local, mesh.shape["col"]),
        mesh=mesh,
        in_specs=placed,
        out_specs=P("col", None, "row", None),
        check_vma=False,
    )
```

```python
import functools

import jax
import jax.numpy as jnp
from jax import lax
from jax.experimental import pallas as pl
from jax.experimental.pallas import tpu as pltpu
from jax.sharding import PartitionSpec as P

MESH = pl.DeviceIdType.MESH
NEAR = 4
STRIDE = 27
LEVELS = 32767.0
LAST = 16


def coded(e):
    top = jnp.maximum(jnp.max(e, axis=0, keepdims=True), 1e-30)
    code = (e * (LEVELS / top) + 0.5).astype(jnp.int32).astype(jnp.int16)
    step = top * (1.0 / LEVELS)
    return code, step * step


def squared(code):
    value = code.astype(jnp.int32).astype(jnp.float32)
    return value * value


def kernel(
    n,
    rows_ref,
    keep_ref,
    hand_ref,
    slot_ref,
    source_ref,
    out_ref,
    tiles_ref,
    full,
    stage_a,
    stage_b,
    arrived_a,
    arrived_b,
    acc,
    sums,
    sums_in,
    steps,
    factors,
    factors_in,
    early,
    early_in,
    late_a,
    late_b,
    late_in_a,
    late_in_b,
    x_send,
    x_recv,
    z_send,
    z_recv,
    s_send,
    s_recv,
    h_send,
    h_recv,
    own_sem,
):
    count, slots, height, width = tiles_ref.shape
    stage, arrived = (stage_a, stage_b), (arrived_a, arrived_b)
    late, late_in = (late_a, late_b), (late_in_a, late_in_b)
    half = count // 2
    parts = ((0, height - LAST), (height - LAST, LAST))
    me = lax.axis_index("col")
    x = lax.axis_index("row")
    up, down, across = lax.rem(x + 1, 4), lax.rem(x + 3, 4), lax.rem(x + 2, 4)
    partner = lax.rem(me + n // 2, n)
    mixed = (0,) + tuple(range(NEAR, slots))
    lag = 2
    ahead = 1
    pairs = count // 2
    groups = count // NEAR
    per = 2 * n // pairs

    held = pltpu.make_async_copy(source_ref, tiles_ref, own_sem.at[0])
    held.start()
    placed = pltpu.make_async_copy(source_ref, full.at[:, x], own_sem.at[1])
    placed.start()

    barrier = pltpu.get_barrier_semaphore()
    for peer in (up, down, across):
        pl.semaphore_signal(barrier, inc=1, device_id={"row": peer}, device_id_type=MESH)

    @pl.loop(1, n)
    def _(t):
        pl.semaphore_signal(
            barrier, inc=1, device_id={"col": lax.rem(me + t, n)}, device_id_type=MESH
        )

    sums[...] = jnp.zeros_like(sums)
    factors[...] = jnp.zeros_like(factors)
    held.wait()
    pl.semaphore_wait(barrier, n + 2)

    def direct(j, way):
        return pltpu.make_async_remote_copy(
            src_ref=tiles_ref.at[j],
            dst_ref=full.at[j, x],
            send_sem=x_send.at[way],
            recv_sem=x_recv.at[way, j],
            device_id={"row": (up, down)[way]},
            device_id_type=MESH,
        )

    def relay(j, way):
        origin = (down, up)[way]
        return pltpu.make_async_remote_copy(
            src_ref=full.at[j, origin],
            dst_ref=full.at[j, origin],
            send_sem=x_send.at[2],
            recv_sem=x_recv.at[2, j],
            device_id={"row": (up, down)[way]},
            device_id_type=MESH,
        )

    def far(h, t):
        return pltpu.make_async_remote_copy(
            src_ref=stage[h].at[t - 1],
            dst_ref=arrived[h].at[t - 1],
            send_sem=z_send.at[h],
            recv_sem=z_recv.at[h],
            device_id={"col": lax.rem(me + t, n)},
            device_id_type=MESH,
        )

    def all_far(h):
        return pltpu.make_async_remote_copy(
            src_ref=stage[h],
            dst_ref=arrived[h],
            send_sem=z_send.at[h],
            recv_sem=z_recv.at[h],
            device_id={"col": partner},
            device_id_type=MESH,
        )

    def all_rows(way):
        return pltpu.make_async_remote_copy(
            src_ref=tiles_ref,
            dst_ref=full.at[:, x],
            send_sem=x_send.at[way],
            recv_sem=x_recv.at[0, 0],
            device_id={"row": up},
            device_id_type=MESH,
        )

    def total(g, k):
        return pltpu.make_async_remote_copy(
            src_ref=sums.at[g],
            dst_ref=sums_in.at[k, g],
            send_sem=s_send.at[k],
            recv_sem=s_recv.at[g, k],
            device_id={"row": (up, down, across)[k]},
            device_id_type=MESH,
        )

    def to_partner(source, target, kind, i):
        return pltpu.make_async_remote_copy(
            src_ref=source,
            dst_ref=target,
            send_sem=h_send.at[kind],
            recv_sem=h_recv.at[kind, i],
            device_id={"col": partner},
            device_id_type=MESH,
        )

    def hand_late(h, j):
        return to_partner(late[h].at[j - half], late_in[h].at[j - half], h, j - half)

    def hand_early(j):
        return to_partner(early.at[j - half], early_in.at[j - half], 2, j - half)

    def hand_factor(j):
        return to_partner(factors.at[j - half], factors_in.at[j - half], 3, j - half)

    def send_far(number):
        i = lax.rem(number, n)
        t = lax.rem(i * STRIDE, n)
        pick = slot_ref[t]
        column = lax.rem(pick, count)
        for h in range(2):

            @pl.when((i > 0) & (number // n == h))
            def _():
                rows = pl.ds(*parts[h])
                stage[h][t - 1, 0] = tiles_ref[column, 0, rows]
                stage[h][t - 1, 1] = tiles_ref[column, NEAR + pick // count, rows]
                far(h, t).start()

    @pl.loop(0, lag)
    def _(p):
        for k in range(2):
            for way in range(2):
                direct(count - 1 - k - 2 * p, way).start()

                @pl.when(p < ahead)
                def _():
                    @pl.loop(0, per // 4)
                    def _(m):
                        send_far(p * per + (2 * k + way) * (per // 4) + m)

    placed.wait()

    def right(j, s):
        return full[j, :, s].reshape(4 * height, width)

    def row_of(ref, j):
        return ref[j // NEAR, pl.ds(lax.rem(j, NEAR), 1), :]

    def set_row(ref, j, value):
        ref[j // NEAR, pl.ds(lax.rem(j, NEAR), 1), :] = value

    def near(j, hands):
        left = []
        for s in range(NEAR):
            column = j if s == 0 else lax.rem(rows_ref[s, j], count)
            left.append(
                jnp.concatenate([tiles_ref[column, q ^ s] for q in range(NEAR)], axis=0)
            )
        a = jnp.concatenate(left, axis=1)
        b = jnp.concatenate([right(j, s) for s in range(NEAR)], axis=0)
        p = jnp.dot(a, b, preferred_element_type=jnp.float32).reshape(NEAR, height, width)
        acc[j, 0] = p[0]
        column_sum = jnp.zeros((1, width), jnp.float32)
        for q in range(1, NEAR):
            e = p[q] * keep_ref[q, j].astype(jnp.float32)
            if hands:
                early[j - half, q - 1], step = coded(e)
                steps[j - half, q - 1 : q, :] = step
            e = e * e
            acc[j, q] = e
            column_sum = column_sum + jnp.sum(e, axis=0, keepdims=True)
        set_row(sums, j, column_sum)
        c = tiles_ref[j, NEAR:].reshape((slots - NEAR) * height, width)
        acc[j, NEAR:] = jnp.dot(c, right(j, 0), preferred_element_type=jnp.float32).reshape(
            slots - NEAR, height, width
        )
        if hands:
            hand_early(j).start()

    def expand(h, columns, hands):
        halves = (0, 1) if h is None else (h,)
        edge = sum(parts[i][1] for i in halves)
        rows = pl.ds(parts[halves[0]][0], edge)
        products = []
        for j in columns:
            for s in range(NEAR, slots):
                t = lax.rem(me - rows_ref[s, j] // count + n, n)
                a = jnp.concatenate(
                    [arrived[i][jnp.maximum(t - 1, 0), k] for k in range(2) for i in halves], axis=0
                )
                products.append(jnp.dot(a, right(j, s), preferred_element_type=jnp.float32))
        for c, j in enumerate(columns):
            mine = products[c * (slots - NEAR) : (c + 1) * (slots - NEAR)]
            own = acc[j, 0, rows]
            for p in mine:
                own = own + p[edge:]
            values = [own] + [acc[j, NEAR + i, rows] + p[:edge] for i, p in enumerate(mine)]
            column_sum = row_of(sums, j)
            for i, q in enumerate(mixed):
                e = values[i] * keep_ref[q, j].astype(jnp.float32)
                if hands:
                    late[h][j - half, i], step = coded(e)
                    r = NEAR - 1 + h * len(mixed) + i
                    steps[j - half, r : r + 1, :] = step
                e = e * e
                acc[j, q, rows] = e
                column_sum = column_sum + jnp.sum(e, axis=0, keepdims=True)
            set_row(sums, j, column_sum)
            if hands:
                hand_late(h, j).start()

    def scale_of(j):
        whole = row_of(sums, j)
        for k in range(3):
            whole = whole + row_of(sums_in.at[k], j)
        return width / whole

    def pass_on(p):
        for k in range(2):
            j = count - 1 - k - 2 * p
            direct(j, k).wait_recv()
            relay(j, k).start()
            for way in range(2):

                @pl.when(p + lag < pairs)
                def _():
                    direct(j - 2 * lag, way).start()

                @pl.loop(0, per // 4)
                def _(m):
                    send_far((p + ahead) * per + (2 * k + way) * (per // 4) + m)

    def near_pair(p, hands):
        for k in range(2):
            j = count - 1 - k - 2 * p
            direct(j, 1 - k).wait_recv()
            relay(j, k).wait_recv()
            near(j, hands)

    def await_far(h):
        all_far(h).wait_recv()

    def expand_all(h, first, last, hands):
        @pl.loop(0, (last - first) // 2)
        def _(i):
            j = last - 1 - 2 * i
            expand(h, (j, j - 1), hands)

    def start_totals(g):
        for k in range(3):
            total(g, k).start()

    def await_totals(g):
        for k in range(3):
            total(g, k).wait_recv()

    def normalize(g):
        await_totals(g)

        @pl.loop(g * NEAR, (g + 1) * NEAR)
        def _(j):
            scale = scale_of(j)
            for q in range(slots):
                out_ref[j, q] = (acc[j, q] * scale).astype(jnp.bfloat16)

    @pl.loop(0, lag)
    def _(p):
        pass_on(p)

    @pl.loop(lag, pairs // 2 + lag)
    def _(p):
        pass_on(p)
        near_pair(p - lag, True)

    pass_on(6)
    await_far(0)
    expand_all(0, half, count, True)
    near_pair(4, False)
    pass_on(7)
    await_far(1)
    for g in (3, 2):
        expand_all(1, g * NEAR, (g + 1) * NEAR, True)
        start_totals(g)
    near_pair(5, False)
    expand_all(None, NEAR, 2 * NEAR, False)
    start_totals(1)

    for g in (3, 2):
        await_totals(g)

        @pl.loop(g * NEAR, (g + 1) * NEAR)
        def _(j):
            scale = scale_of(j)
            for r in range(NEAR - 1 + 2 * len(mixed)):
                factors[j - half, r : r + 1, :] = steps[j - half, r : r + 1, :] * scale
            hand_factor(j).start()

    near_pair(6, False)
    expand(None, (3, 2), False)
    normalize(1)
    near_pair(7, False)
    expand(None, (1, 0), False)
    start_totals(0)

    first = count - hand_ref[0]

    @pl.loop(0, half)
    def _(i):
        j = count - 1 - i
        hand_factor(j).wait_recv()
        hand_early(j).wait_recv()
        for h in range(2):
            hand_late(h, j).wait_recv()
        scale = scale_of(j)
        take = jnp.full((height, width), j, jnp.int32) >= first
        for q in range(1, NEAR):
            theirs = squared(early_in[j - half, q - 1]) * factors_in[j - half, q - 1 : q, :]
            out_ref[j, q] = jnp.where(take, theirs, acc[j, q] * scale).astype(jnp.bfloat16)
        for i, q in enumerate(mixed):
            for h in range(2):
                rows = pl.ds(*parts[h])
                r = NEAR - 1 + h * len(mixed) + i
                theirs = squared(late_in[h][j - half, i]) * factors_in[j - half, r : r + 1, :]
                out_ref[j, q, rows] = jnp.where(
                    take[: parts[h][1]], theirs, acc[j, q, rows] * scale
                ).astype(jnp.bfloat16)

    normalize(0)

    for way in range(3):
        all_rows(way).wait_send()
    for h in range(2):
        all_far(h).wait_send()
        to_partner(late[h], late_in[h], h, 0).wait_send()
    to_partner(early, early_in, 2, 0).wait_send()
    to_partner(factors, factors_in, 3, 0).wait_send()
    for k in range(3):
        pltpu.make_async_remote_copy(
            src_ref=sums,
            dst_ref=sums_in.at[k],
            send_sem=s_send.at[k],
            recv_sem=s_recv.at[0, k],
            device_id={"row": up},
            device_id_type=MESH,
        ).wait_send()


def local(n, tiles, tile_rows, keep, hand):
    count, slots, height, width = tiles.shape
    half = count // 2
    groups = count // NEAR
    far_count = slots - NEAR
    me = lax.axis_index("col")
    tile_rows = tile_rows.T
    owner = tile_rows[NEAR:] // count
    shift = (owner - me + n) % n
    request = jnp.arange(far_count * count, dtype=jnp.int32).reshape(far_count, count)
    turn = jnp.arange(n, dtype=jnp.int32)[:, None, None]
    slot = jnp.sum(jnp.where(shift[None] == turn, request[None], 0), (1, 2))
    smem = pl.BlockSpec(memory_space=pltpu.SMEM)
    vmem = pl.BlockSpec(memory_space=pltpu.VMEM)
    dma = pltpu.SemaphoreType.DMA
    return pl.pallas_call(
        functools.partial(kernel, n),
        out_shape=pltpu.VMEM(tiles.shape, tiles.dtype),
        in_specs=[smem, smem, smem, smem, pl.BlockSpec(memory_space=pl.ANY)],
        out_specs=vmem,
        scratch_shapes=[
            pltpu.VMEM(tiles.shape, tiles.dtype),
            pltpu.VMEM((count, 4, slots, height, width), jnp.bfloat16),
            pltpu.VMEM((n - 1, 2, height - LAST, width), jnp.bfloat16),
            pltpu.VMEM((n - 1, 2, LAST, width), jnp.bfloat16),
            pltpu.VMEM((n - 1, 2, height - LAST, width), jnp.bfloat16),
            pltpu.VMEM((n - 1, 2, LAST, width), jnp.bfloat16),
            pltpu.VMEM((count, slots, height, width), jnp.float32),
            pltpu.VMEM((groups, 8, width), jnp.float32),
            pltpu.VMEM((3, groups, 8, width), jnp.float32),
            pltpu.VMEM((half, 16, width), jnp.float32),
            pltpu.VMEM((half, 16, width), jnp.float32),
            pltpu.VMEM((half, 16, width), jnp.float32),
            pltpu.VMEM((half, NEAR - 1, height, width), jnp.int16),
            pltpu.VMEM((half, NEAR - 1, height, width), jnp.int16),
            pltpu.VMEM((half, 1 + far_count, height - LAST, width), jnp.int16),
            pltpu.VMEM((half, 1 + far_count, LAST, width), jnp.int16),
            pltpu.VMEM((half, 1 + far_count, height - LAST, width), jnp.int16),
            pltpu.VMEM((half, 1 + far_count, LAST, width), jnp.int16),
            dma((3,)),
            dma((3, count)),
            dma((2,)),
            dma((2,)),
            dma((3,)),
            dma((groups, 3)),
            dma((4,)),
            dma((4, half)),
            dma((2,)),
        ],
        compiler_params=pltpu.CompilerParams(
            collective_id=0, has_side_effects=True, vmem_limit_bytes=56 * 1024 * 1024
        ),
        cost_estimate=pl.CostEstimate(
            flops=22 * 2 * count * height * 4 * height * width,
            bytes_accessed=2 * tiles.size * 2,
            transcendentals=0,
        ),
    )(tile_rows, keep.T, hand, slot, tiles)


def solution(mesh):
    placed = (P("col", None, "row", None), P("col", None), P("col", None), P("col"))
    return jax.shard_map(
        functools.partial(local, mesh.shape["col"]),
        mesh=mesh,
        in_specs=placed,
        out_specs=P("col", None, "row", None),
        check_vma=False,
    )
```

```python
import functools

import jax
import jax.numpy as jnp
from jax import lax
from jax.experimental import pallas as pl
from jax.experimental.pallas import tpu as pltpu
from jax.sharding import PartitionSpec as P

MESH = pl.DeviceIdType.MESH
NEAR = 4
STRIDE = 27
LEVELS = 32767.0
LAST = 16


def coded(e):
    top = jnp.maximum(jnp.max(e, axis=0, keepdims=True), 1e-30)
    code = (e * (LEVELS / top) + 0.5).astype(jnp.int32).astype(jnp.int16)
    step = top * (1.0 / LEVELS)
    return code, step * step


def squared(code):
    value = code.astype(jnp.int32).astype(jnp.float32)
    return value * value


def kernel(
    n,
    rows_ref,
    keep_ref,
    hand_ref,
    slot_ref,
    source_ref,
    out_ref,
    tiles_ref,
    full,
    stage_a,
    stage_b,
    arrived_a,
    arrived_b,
    acc,
    sums,
    sums_in,
    steps,
    factors,
    factors_in,
    early,
    early_in,
    late_a,
    late_b,
    late_in_a,
    late_in_b,
    x_send,
    x_recv,
    z_send,
    z_recv,
    s_send,
    s_recv,
    h_send,
    h_recv,
    own_sem,
):
    count, slots, height, width = tiles_ref.shape
    stage, arrived = (stage_a, stage_b), (arrived_a, arrived_b)
    late, late_in = (late_a, late_b), (late_in_a, late_in_b)
    half = count // 2
    parts = ((0, height - LAST), (height - LAST, LAST))
    me = lax.axis_index("col")
    x = lax.axis_index("row")
    up, down, across = lax.rem(x + 1, 4), lax.rem(x + 3, 4), lax.rem(x + 2, 4)
    partner = lax.rem(me + n // 2, n)
    mixed = (0,) + tuple(range(NEAR, slots))
    lag = 2
    ahead = 1
    pairs = count // 2
    groups = count // NEAR
    per = 2 * n // pairs

    held = pltpu.make_async_copy(source_ref, tiles_ref, own_sem.at[0])
    held.start()
    placed = pltpu.make_async_copy(source_ref, full.at[:, x], own_sem.at[1])
    placed.start()

    barrier = pltpu.get_barrier_semaphore()
    for peer in (up, down, across):
        pl.semaphore_signal(barrier, inc=1, device_id={"row": peer}, device_id_type=MESH)

    @pl.loop(1, n)
    def _(t):
        pl.semaphore_signal(
            barrier, inc=1, device_id={"col": lax.rem(me + t, n)}, device_id_type=MESH
        )

    sums[...] = jnp.zeros_like(sums)
    factors[...] = jnp.zeros_like(factors)
    held.wait()
    pl.semaphore_wait(barrier, n + 2)

    def direct(j, way):
        return pltpu.make_async_remote_copy(
            src_ref=tiles_ref.at[j],
            dst_ref=full.at[j, x],
            send_sem=x_send.at[way],
            recv_sem=x_recv.at[way, j],
            device_id={"row": (up, down)[way]},
            device_id_type=MESH,
        )

    def relay(j, way):
        origin = (down, up)[way]
        return pltpu.make_async_remote_copy(
            src_ref=full.at[j, origin],
            dst_ref=full.at[j, origin],
            send_sem=x_send.at[2],
            recv_sem=x_recv.at[2, j],
            device_id={"row": (up, down)[way]},
            device_id_type=MESH,
        )

    def far(h, t):
        return pltpu.make_async_remote_copy(
            src_ref=stage[h].at[t - 1],
            dst_ref=arrived[h].at[t - 1],
            send_sem=z_send.at[h],
            recv_sem=z_recv.at[h],
            device_id={"col": lax.rem(me + t, n)},
            device_id_type=MESH,
        )

    def all_far(h):
        return pltpu.make_async_remote_copy(
            src_ref=stage[h],
            dst_ref=arrived[h],
            send_sem=z_send.at[h],
            recv_sem=z_recv.at[h],
            device_id={"col": partner},
            device_id_type=MESH,
        )

    def all_rows(way):
        return pltpu.make_async_remote_copy(
            src_ref=tiles_ref,
            dst_ref=full.at[:, x],
            send_sem=x_send.at[way],
            recv_sem=x_recv.at[0, 0],
            device_id={"row": up},
            device_id_type=MESH,
        )

    def total(g, k):
        return pltpu.make_async_remote_copy(
            src_ref=sums.at[g],
            dst_ref=sums_in.at[k, g],
            send_sem=s_send.at[k],
            recv_sem=s_recv.at[g, k],
            device_id={"row": (up, down, across)[k]},
            device_id_type=MESH,
        )

    def to_partner(source, target, kind, i):
        return pltpu.make_async_remote_copy(
            src_ref=source,
            dst_ref=target,
            send_sem=h_send.at[kind],
            recv_sem=h_recv.at[kind, i],
            device_id={"col": partner},
            device_id_type=MESH,
        )

    def hand_late(h, j):
        return to_partner(late[h].at[j - half], late_in[h].at[j - half], h, j - half)

    def hand_early(j):
        return to_partner(early.at[j - half], early_in.at[j - half], 2, j - half)

    def hand_factor(j):
        return to_partner(factors.at[j - half], factors_in.at[j - half], 3, j - half)

    def send_far(number):
        i = lax.rem(number, n)
        t = lax.rem(i * STRIDE, n)
        pick = slot_ref[t]
        column = lax.rem(pick, count)
        for h in range(2):

            @pl.when((i > 0) & (number // n == h))
            def _():
                rows = pl.ds(*parts[h])
                stage[h][t - 1, 0] = tiles_ref[column, 0, rows]
                stage[h][t - 1, 1] = tiles_ref[column, NEAR + pick // count, rows]
                far(h, t).start()

    @pl.loop(0, lag)
    def _(p):
        for k in range(2):
            for way in range(2):
                direct(count - 1 - k - 2 * p, way).start()

                @pl.when(p < ahead)
                def _():
                    @pl.loop(0, per // 4)
                    def _(m):
                        send_far(p * per + (2 * k + way) * (per // 4) + m)

    placed.wait()

    def right(j, s):
        return full[j, :, s].reshape(4 * height, width)

    def row_of(ref, j):
        return ref[j // NEAR, pl.ds(lax.rem(j, NEAR), 1), :]

    def set_row(ref, j, value):
        ref[j // NEAR, pl.ds(lax.rem(j, NEAR), 1), :] = value

    def near(j, hands):
        left = []
        for s in range(NEAR):
            column = j if s == 0 else lax.rem(rows_ref[s, j], count)
            left.append(
                jnp.concatenate([tiles_ref[column, q ^ s] for q in range(NEAR)], axis=0)
            )
        a = jnp.concatenate(left, axis=1)
        b = jnp.concatenate([right(j, s) for s in range(NEAR)], axis=0)
        p = jnp.dot(a, b, preferred_element_type=jnp.float32).reshape(NEAR, height, width)
        acc[j, 0] = p[0]
        column_sum = jnp.zeros((1, width), jnp.float32)
        for q in range(1, NEAR):
            e = p[q] * keep_ref[q, j].astype(jnp.float32)
            if hands:
                early[j - half, q - 1], step = coded(e)
                steps[j - half, q - 1 : q, :] = step
            e = e * e
            acc[j, q] = e
            column_sum = column_sum + jnp.sum(e, axis=0, keepdims=True)
        set_row(sums, j, column_sum)
        c = tiles_ref[j, NEAR:].reshape((slots - NEAR) * height, width)
        acc[j, NEAR:] = jnp.dot(c, right(j, 0), preferred_element_type=jnp.float32).reshape(
            slots - NEAR, height, width
        )
        if hands:
            hand_early(j).start()

    def expand(h, columns, hands):
        halves = (0, 1) if h is None else (h,)
        edge = sum(parts[i][1] for i in halves)
        rows = pl.ds(parts[halves[0]][0], edge)
        products = []
        for j in columns:
            for s in range(NEAR, slots):
                t = lax.rem(me - rows_ref[s, j] // count + n, n)
                a = jnp.concatenate(
                    [arrived[i][jnp.maximum(t - 1, 0), k] for k in range(2) for i in halves], axis=0
                )
                products.append(jnp.dot(a, right(j, s), preferred_element_type=jnp.float32))
        for c, j in enumerate(columns):
            mine = products[c * (slots - NEAR) : (c + 1) * (slots - NEAR)]
            own = acc[j, 0, rows]
            for p in mine:
                own = own + p[edge:]
            values = [own] + [acc[j, NEAR + i, rows] + p[:edge] for i, p in enumerate(mine)]
            column_sum = row_of(sums, j)
            for i, q in enumerate(mixed):
                e = values[i] * keep_ref[q, j].astype(jnp.float32)
                if hands:
                    late[h][j - half, i], step = coded(e)
                    r = NEAR - 1 + h * len(mixed) + i
                    steps[j - half, r : r + 1, :] = step
                e = e * e
                acc[j, q, rows] = e
                column_sum = column_sum + jnp.sum(e, axis=0, keepdims=True)
            set_row(sums, j, column_sum)
            if hands:
                hand_late(h, j).start()

    def scale_of(j):
        whole = row_of(sums, j)
        for k in range(3):
            whole = whole + row_of(sums_in.at[k], j)
        return width / whole

    def pass_on(p):
        for k in range(2):
            j = count - 1 - k - 2 * p
            direct(j, k).wait_recv()
            relay(j, k).start()
            for way in range(2):

                @pl.when(p + lag < pairs)
                def _():
                    direct(j - 2 * lag, way).start()

                @pl.loop(0, per // 4)
                def _(m):
                    send_far((p + ahead) * per + (2 * k + way) * (per // 4) + m)

    def near_pair(p, hands):
        for k in range(2):
            j = count - 1 - k - 2 * p
            direct(j, 1 - k).wait_recv()
            relay(j, k).wait_recv()
            near(j, hands)

    def await_far(h):
        all_far(h).wait_recv()

    def expand_all(h, first, last, hands):
        @pl.loop(0, (last - first) // 2)
        def _(i):
            j = last - 1 - 2 * i
            expand(h, (j, j - 1), hands)

    def start_totals(g):
        for k in range(3):
            total(g, k).start()

    def await_totals(g):
        for k in range(3):
            total(g, k).wait_recv()

    def normalize(g):
        await_totals(g)

        @pl.loop(g * NEAR, (g + 1) * NEAR)
        def _(j):
            scale = scale_of(j)
            for q in range(slots):
                out_ref[j, q] = (acc[j, q] * scale).astype(jnp.bfloat16)

    @pl.loop(0, lag)
    def _(p):
        pass_on(p)

    @pl.loop(lag, pairs // 2 + lag)
    def _(p):
        pass_on(p)
        near_pair(p - lag, True)

    pass_on(6)
    await_far(0)
    expand_all(0, half, count, True)
    near_pair(4, False)
    pass_on(7)
    await_far(1)
    for g in (3, 2):
        expand_all(1, g * NEAR, (g + 1) * NEAR, True)
        start_totals(g)

    for g in (3, 2):
        await_totals(g)

        @pl.loop(g * NEAR, (g + 1) * NEAR)
        def _(j):
            scale = scale_of(j)
            for r in range(NEAR - 1 + 2 * len(mixed)):
                factors[j - half, r : r + 1, :] = steps[j - half, r : r + 1, :] * scale
            hand_factor(j).start()

    near_pair(5, False)
    expand_all(None, NEAR, 2 * NEAR, False)
    start_totals(1)

    near_pair(6, False)
    expand(None, (3, 2), False)
    normalize(1)
    near_pair(7, False)
    expand(None, (1, 0), False)
    start_totals(0)

    first = count - hand_ref[0]

    @pl.loop(0, half)
    def _(i):
        j = count - 1 - i
        hand_factor(j).wait_recv()
        hand_early(j).wait_recv()
        for h in range(2):
            hand_late(h, j).wait_recv()
        scale = scale_of(j)
        take = jnp.full((height, width), j, jnp.int32) >= first
        for q in range(1, NEAR):
            theirs = squared(early_in[j - half, q - 1]) * factors_in[j - half, q - 1 : q, :]
            out_ref[j, q] = jnp.where(take, theirs, acc[j, q] * scale).astype(jnp.bfloat16)
        for i, q in enumerate(mixed):
            for h in range(2):
                rows = pl.ds(*parts[h])
                r = NEAR - 1 + h * len(mixed) + i
                theirs = squared(late_in[h][j - half, i]) * factors_in[j - half, r : r + 1, :]
                out_ref[j, q, rows] = jnp.where(
                    take[: parts[h][1]], theirs, acc[j, q, rows] * scale
                ).astype(jnp.bfloat16)

    normalize(0)

    for way in range(3):
        all_rows(way).wait_send()
    for h in range(2):
        all_far(h).wait_send()
        to_partner(late[h], late_in[h], h, 0).wait_send()
    to_partner(early, early_in, 2, 0).wait_send()
    to_partner(factors, factors_in, 3, 0).wait_send()
    for k in range(3):
        pltpu.make_async_remote_copy(
            src_ref=sums,
            dst_ref=sums_in.at[k],
            send_sem=s_send.at[k],
            recv_sem=s_recv.at[0, k],
            device_id={"row": up},
            device_id_type=MESH,
        ).wait_send()


def local(n, tiles, tile_rows, keep, hand):
    count, slots, height, width = tiles.shape
    half = count // 2
    groups = count // NEAR
    far_count = slots - NEAR
    me = lax.axis_index("col")
    tile_rows = tile_rows.T
    owner = tile_rows[NEAR:] // count
    shift = (owner - me + n) % n
    request = jnp.arange(far_count * count, dtype=jnp.int32).reshape(far_count, count)
    turn = jnp.arange(n, dtype=jnp.int32)[:, None, None]
    slot = jnp.sum(jnp.where(shift[None] == turn, request[None], 0), (1, 2))
    smem = pl.BlockSpec(memory_space=pltpu.SMEM)
    vmem = pl.BlockSpec(memory_space=pltpu.VMEM)
    dma = pltpu.SemaphoreType.DMA
    return pl.pallas_call(
        functools.partial(kernel, n),
        out_shape=pltpu.VMEM(tiles.shape, tiles.dtype),
        in_specs=[smem, smem, smem, smem, pl.BlockSpec(memory_space=pl.ANY)],
        out_specs=vmem,
        scratch_shapes=[
            pltpu.VMEM(tiles.shape, tiles.dtype),
            pltpu.VMEM((count, 4, slots, height, width), jnp.bfloat16),
            pltpu.VMEM((n - 1, 2, height - LAST, width), jnp.bfloat16),
            pltpu.VMEM((n - 1, 2, LAST, width), jnp.bfloat16),
            pltpu.VMEM((n - 1, 2, height - LAST, width), jnp.bfloat16),
            pltpu.VMEM((n - 1, 2, LAST, width), jnp.bfloat16),
            pltpu.VMEM((count, slots, height, width), jnp.float32),
            pltpu.VMEM((groups, 8, width), jnp.float32),
            pltpu.VMEM((3, groups, 8, width), jnp.float32),
            pltpu.VMEM((half, 16, width), jnp.float32),
            pltpu.VMEM((half, 16, width), jnp.float32),
            pltpu.VMEM((half, 16, width), jnp.float32),
            pltpu.VMEM((half, NEAR - 1, height, width), jnp.int16),
            pltpu.VMEM((half, NEAR - 1, height, width), jnp.int16),
            pltpu.VMEM((half, 1 + far_count, height - LAST, width), jnp.int16),
            pltpu.VMEM((half, 1 + far_count, LAST, width), jnp.int16),
            pltpu.VMEM((half, 1 + far_count, height - LAST, width), jnp.int16),
            pltpu.VMEM((half, 1 + far_count, LAST, width), jnp.int16),
            dma((3,)),
            dma((3, count)),
            dma((2,)),
            dma((2,)),
            dma((3,)),
            dma((groups, 3)),
            dma((4,)),
            dma((4, half)),
            dma((2,)),
        ],
        compiler_params=pltpu.CompilerParams(
            collective_id=0, has_side_effects=True, vmem_limit_bytes=56 * 1024 * 1024
        ),
        cost_estimate=pl.CostEstimate(
            flops=22 * 2 * count * height * 4 * height * width,
            bytes_accessed=2 * tiles.size * 2,
            transcendentals=0,
        ),
    )(tile_rows, keep.T, hand, slot, tiles)


def solution(mesh):
    placed = (P("col", None, "row", None), P("col", None), P("col", None), P("col"))
    return jax.shard_map(
        functools.partial(local, mesh.shape["col"]),
        mesh=mesh,
        in_specs=placed,
        out_specs=P("col", None, "row", None),
        check_vma=False,
    )
```

```python
import functools

import jax
import jax.numpy as jnp
from jax import lax
from jax.experimental import pallas as pl
from jax.experimental.pallas import tpu as pltpu
from jax.sharding import PartitionSpec as P

MESH = pl.DeviceIdType.MESH
NEAR = 4
STRIDE = 27
LEVELS = 32767.0
LAST = 16


def coded(e):
    top = jnp.maximum(jnp.max(e, axis=0, keepdims=True), 1e-30)
    code = (e * (LEVELS / top) + 0.5).astype(jnp.int32).astype(jnp.int16)
    step = top * (1.0 / LEVELS)
    return code, step * step


def squared(code):
    value = code.astype(jnp.int32).astype(jnp.float32)
    return value * value


def kernel(
    n,
    rows_ref,
    keep_ref,
    hand_ref,
    slot_ref,
    source_ref,
    out_ref,
    tiles_ref,
    full,
    stage_a,
    stage_b,
    arrived_a,
    arrived_b,
    acc,
    sums,
    sums_in,
    steps,
    factors,
    factors_in,
    early,
    early_in,
    late_a,
    late_b,
    late_in_a,
    late_in_b,
    x_send,
    x_recv,
    z_send,
    z_recv,
    s_send,
    s_recv,
    h_send,
    h_recv,
    own_sem,
):
    count, slots, height, width = tiles_ref.shape
    stage, arrived = (stage_a, stage_b), (arrived_a, arrived_b)
    late, late_in = (late_a, late_b), (late_in_a, late_in_b)
    half = count // 2
    parts = ((0, height - LAST), (height - LAST, LAST))
    me = lax.axis_index("col")
    x = lax.axis_index("row")
    up, down, across = lax.rem(x + 1, 4), lax.rem(x + 3, 4), lax.rem(x + 2, 4)
    partner = lax.rem(me + n // 2, n)
    mixed = (0,) + tuple(range(NEAR, slots))
    lag = 2
    ahead = 2
    pairs = count // 2
    groups = count // NEAR
    per = 2 * n // pairs

    held = pltpu.make_async_copy(source_ref, tiles_ref, own_sem.at[0])
    held.start()
    placed = pltpu.make_async_copy(source_ref, full.at[:, x], own_sem.at[1])
    placed.start()

    barrier = pltpu.get_barrier_semaphore()
    for peer in (up, down, across):
        pl.semaphore_signal(barrier, inc=1, device_id={"row": peer}, device_id_type=MESH)

    @pl.loop(1, n)
    def _(t):
        pl.semaphore_signal(
            barrier, inc=1, device_id={"col": lax.rem(me + t, n)}, device_id_type=MESH
        )

    sums[...] = jnp.zeros_like(sums)
    factors[...] = jnp.zeros_like(factors)
    held.wait()
    pl.semaphore_wait(barrier, n + 2)

    def direct(j, way):
        return pltpu.make_async_remote_copy(
            src_ref=tiles_ref.at[j],
            dst_ref=full.at[j, x],
            send_sem=x_send.at[way],
            recv_sem=x_recv.at[way, j],
            device_id={"row": (up, down)[way]},
            device_id_type=MESH,
        )

    def relay(j, way):
        origin = (down, up)[way]
        return pltpu.make_async_remote_copy(
            src_ref=full.at[j, origin],
            dst_ref=full.at[j, origin],
            send_sem=x_send.at[2],
            recv_sem=x_recv.at[2, j],
            device_id={"row": (up, down)[way]},
            device_id_type=MESH,
        )

    def far(h, t):
        return pltpu.make_async_remote_copy(
            src_ref=stage[h].at[t - 1],
            dst_ref=arrived[h].at[t - 1],
            send_sem=z_send.at[h],
            recv_sem=z_recv.at[h],
            device_id={"col": lax.rem(me + t, n)},
            device_id_type=MESH,
        )

    def all_far(h):
        return pltpu.make_async_remote_copy(
            src_ref=stage[h],
            dst_ref=arrived[h],
            send_sem=z_send.at[h],
            recv_sem=z_recv.at[h],
            device_id={"col": partner},
            device_id_type=MESH,
        )

    def all_rows(way):
        return pltpu.make_async_remote_copy(
            src_ref=tiles_ref,
            dst_ref=full.at[:, x],
            send_sem=x_send.at[way],
            recv_sem=x_recv.at[0, 0],
            device_id={"row": up},
            device_id_type=MESH,
        )

    def total(g, k):
        return pltpu.make_async_remote_copy(
            src_ref=sums.at[g],
            dst_ref=sums_in.at[k, g],
            send_sem=s_send.at[k],
            recv_sem=s_recv.at[g, k],
            device_id={"row": (up, down, across)[k]},
            device_id_type=MESH,
        )

    def to_partner(source, target, kind, i):
        return pltpu.make_async_remote_copy(
            src_ref=source,
            dst_ref=target,
            send_sem=h_send.at[kind],
            recv_sem=h_recv.at[kind, i],
            device_id={"col": partner},
            device_id_type=MESH,
        )

    def hand_late(h, j):
        return to_partner(late[h].at[j - half], late_in[h].at[j - half], h, j - half)

    def hand_early(j):
        return to_partner(early.at[j - half], early_in.at[j - half], 2, j - half)

    def hand_factor(j):
        return to_partner(factors.at[j - half], factors_in.at[j - half], 3, j - half)

    def send_far(number):
        i = lax.rem(number, n)
        t = lax.rem(i * STRIDE, n)
        pick = slot_ref[t]
        column = lax.rem(pick, count)
        for h in range(2):

            @pl.when((i > 0) & (number // n == h))
            def _():
                rows = pl.ds(*parts[h])
                stage[h][t - 1, 0] = tiles_ref[column, 0, rows]
                stage[h][t - 1, 1] = tiles_ref[column, NEAR + pick // count, rows]
                far(h, t).start()

    @pl.loop(0, lag)
    def _(p):
        for k in range(2):
            for way in range(2):
                direct(count - 1 - k - 2 * p, way).start()

                @pl.loop(0, per // 4)
                def _(m):
                    send_far(p * per + (2 * k + way) * (per // 4) + m)

    @pl.loop(lag * per, ahead * per)
    def _(number):
        send_far(number)

    placed.wait()

    def right(j, s):
        return full[j, :, s].reshape(4 * height, width)

    def row_of(ref, j):
        return ref[j // NEAR, pl.ds(lax.rem(j, NEAR), 1), :]

    def set_row(ref, j, value):
        ref[j // NEAR, pl.ds(lax.rem(j, NEAR), 1), :] = value

    def near(j, hands):
        left = []
        for s in range(NEAR):
            column = j if s == 0 else lax.rem(rows_ref[s, j], count)
            left.append(
                jnp.concatenate([tiles_ref[column, q ^ s] for q in range(NEAR)], axis=0)
            )
        a = jnp.concatenate(left, axis=1)
        b = jnp.concatenate([right(j, s) for s in range(NEAR)], axis=0)
        p = jnp.dot(a, b, preferred_element_type=jnp.float32).reshape(NEAR, height, width)
        acc[j, 0] = p[0]
        column_sum = jnp.zeros((1, width), jnp.float32)
        for q in range(1, NEAR):
            e = p[q] * keep_ref[q, j].astype(jnp.float32)
            if hands:
                early[j - half, q - 1], step = coded(e)
                steps[j - half, q - 1 : q, :] = step
            e = e * e
            acc[j, q] = e
            column_sum = column_sum + jnp.sum(e, axis=0, keepdims=True)
        set_row(sums, j, column_sum)
        c = tiles_ref[j, NEAR:].reshape((slots - NEAR) * height, width)
        acc[j, NEAR:] = jnp.dot(c, right(j, 0), preferred_element_type=jnp.float32).reshape(
            slots - NEAR, height, width
        )
        if hands:
            hand_early(j).start()

    def expand(h, columns, hands):
        halves = (0, 1) if h is None else (h,)
        edge = sum(parts[i][1] for i in halves)
        rows = pl.ds(parts[halves[0]][0], edge)
        products = []
        for j in columns:
            for s in range(NEAR, slots):
                t = lax.rem(me - rows_ref[s, j] // count + n, n)
                a = jnp.concatenate(
                    [arrived[i][jnp.maximum(t - 1, 0), k] for k in range(2) for i in halves], axis=0
                )
                products.append(jnp.dot(a, right(j, s), preferred_element_type=jnp.float32))
        for c, j in enumerate(columns):
            mine = products[c * (slots - NEAR) : (c + 1) * (slots - NEAR)]
            own = acc[j, 0, rows]
            for p in mine:
                own = own + p[edge:]
            values = [own] + [acc[j, NEAR + i, rows] + p[:edge] for i, p in enumerate(mine)]
            column_sum = row_of(sums, j)
            for i, q in enumerate(mixed):
                e = values[i] * keep_ref[q, j].astype(jnp.float32)
                if hands:
                    late[h][j - half, i], step = coded(e)
                    r = NEAR - 1 + h * len(mixed) + i
                    steps[j - half, r : r + 1, :] = step
                e = e * e
                acc[j, q, rows] = e
                column_sum = column_sum + jnp.sum(e, axis=0, keepdims=True)
            set_row(sums, j, column_sum)
            if hands:
                hand_late(h, j).start()

    def scale_of(j):
        whole = row_of(sums, j)
        for k in range(3):
            whole = whole + row_of(sums_in.at[k], j)
        return width / whole

    def pass_on(p):
        for k in range(2):
            j = count - 1 - k - 2 * p
            direct(j, k).wait_recv()
            relay(j, k).start()
            for way in range(2):

                @pl.when(p + lag < pairs)
                def _():
                    direct(j - 2 * lag, way).start()

                @pl.loop(0, per // 4)
                def _(m):
                    send_far((p + ahead) * per + (2 * k + way) * (per // 4) + m)

    def near_pair(p, hands):
        for k in range(2):
            j = count - 1 - k - 2 * p
            direct(j, 1 - k).wait_recv()
            relay(j, k).wait_recv()
            near(j, hands)

    def await_far(h):
        all_far(h).wait_recv()

    def expand_all(h, first, last, hands):
        @pl.loop(0, (last - first) // 2)
        def _(i):
            j = last - 1 - 2 * i
            expand(h, (j, j - 1), hands)

    def start_totals(g):
        for k in range(3):
            total(g, k).start()

    def await_totals(g):
        for k in range(3):
            total(g, k).wait_recv()

    def normalize(g):
        await_totals(g)

        @pl.loop(g * NEAR, (g + 1) * NEAR)
        def _(j):
            scale = scale_of(j)
            for q in range(slots):
                out_ref[j, q] = (acc[j, q] * scale).astype(jnp.bfloat16)

    @pl.loop(0, lag)
    def _(p):
        pass_on(p)

    @pl.loop(lag, pairs // 2 + lag)
    def _(p):
        pass_on(p)
        near_pair(p - lag, True)

    pass_on(6)
    await_far(0)
    expand_all(0, half, count, True)
    near_pair(4, False)
    pass_on(7)
    await_far(1)
    for g in (3, 2):
        expand_all(1, g * NEAR, (g + 1) * NEAR, True)
        start_totals(g)
    near_pair(5, False)
    expand_all(None, NEAR, 2 * NEAR, False)
    start_totals(1)

    for g in (3, 2):
        await_totals(g)

        @pl.loop(g * NEAR, (g + 1) * NEAR)
        def _(j):
            scale = scale_of(j)
            for r in range(NEAR - 1 + 2 * len(mixed)):
                factors[j - half, r : r + 1, :] = steps[j - half, r : r + 1, :] * scale
            hand_factor(j).start()

    near_pair(6, False)
    expand(None, (3, 2), False)
    near_pair(7, False)
    expand(None, (1, 0), False)
    start_totals(0)
    normalize(1)

    first = count - hand_ref[0]

    @pl.loop(0, half)
    def _(i):
        j = count - 1 - i
        hand_factor(j).wait_recv()
        hand_early(j).wait_recv()
        for h in range(2):
            hand_late(h, j).wait_recv()
        scale = scale_of(j)
        take = jnp.full((height, width), j, jnp.int32) >= first
        for q in range(1, NEAR):
            theirs = squared(early_in[j - half, q - 1]) * factors_in[j - half, q - 1 : q, :]
            out_ref[j, q] = jnp.where(take, theirs, acc[j, q] * scale).astype(jnp.bfloat16)
        for i, q in enumerate(mixed):
            for h in range(2):
                rows = pl.ds(*parts[h])
                r = NEAR - 1 + h * len(mixed) + i
                theirs = squared(late_in[h][j - half, i]) * factors_in[j - half, r : r + 1, :]
                out_ref[j, q, rows] = jnp.where(
                    take[: parts[h][1]], theirs, acc[j, q, rows] * scale
                ).astype(jnp.bfloat16)

    normalize(0)

    for way in range(3):
        all_rows(way).wait_send()
    for h in range(2):
        all_far(h).wait_send()
        to_partner(late[h], late_in[h], h, 0).wait_send()
    to_partner(early, early_in, 2, 0).wait_send()
    to_partner(factors, factors_in, 3, 0).wait_send()
    for k in range(3):
        pltpu.make_async_remote_copy(
            src_ref=sums,
            dst_ref=sums_in.at[k],
            send_sem=s_send.at[k],
            recv_sem=s_recv.at[0, k],
            device_id={"row": up},
            device_id_type=MESH,
        ).wait_send()


def local(n, tiles, tile_rows, keep, hand):
    count, slots, height, width = tiles.shape
    half = count // 2
    groups = count // NEAR
    far_count = slots - NEAR
    me = lax.axis_index("col")
    tile_rows = tile_rows.T
    owner = tile_rows[NEAR:] // count
    shift = (owner - me + n) % n
    request = jnp.arange(far_count * count, dtype=jnp.int32).reshape(far_count, count)
    turn = jnp.arange(n, dtype=jnp.int32)[:, None, None]
    slot = jnp.sum(jnp.where(shift[None] == turn, request[None], 0), (1, 2))
    smem = pl.BlockSpec(memory_space=pltpu.SMEM)
    vmem = pl.BlockSpec(memory_space=pltpu.VMEM)
    dma = pltpu.SemaphoreType.DMA
    return pl.pallas_call(
        functools.partial(kernel, n),
        out_shape=pltpu.VMEM(tiles.shape, tiles.dtype),
        in_specs=[smem, smem, smem, smem, pl.BlockSpec(memory_space=pl.ANY)],
        out_specs=vmem,
        scratch_shapes=[
            pltpu.VMEM(tiles.shape, tiles.dtype),
            pltpu.VMEM((count, 4, slots, height, width), jnp.bfloat16),
            pltpu.VMEM((n - 1, 2, height - LAST, width), jnp.bfloat16),
            pltpu.VMEM((n - 1, 2, LAST, width), jnp.bfloat16),
            pltpu.VMEM((n - 1, 2, height - LAST, width), jnp.bfloat16),
            pltpu.VMEM((n - 1, 2, LAST, width), jnp.bfloat16),
            pltpu.VMEM((count, slots, height, width), jnp.float32),
            pltpu.VMEM((groups, 8, width), jnp.float32),
            pltpu.VMEM((3, groups, 8, width), jnp.float32),
            pltpu.VMEM((half, 16, width), jnp.float32),
            pltpu.VMEM((half, 16, width), jnp.float32),
            pltpu.VMEM((half, 16, width), jnp.float32),
            pltpu.VMEM((half, NEAR - 1, height, width), jnp.int16),
            pltpu.VMEM((half, NEAR - 1, height, width), jnp.int16),
            pltpu.VMEM((half, 1 + far_count, height - LAST, width), jnp.int16),
            pltpu.VMEM((half, 1 + far_count, LAST, width), jnp.int16),
            pltpu.VMEM((half, 1 + far_count, height - LAST, width), jnp.int16),
            pltpu.VMEM((half, 1 + far_count, LAST, width), jnp.int16),
            dma((3,)),
            dma((3, count)),
            dma((2,)),
            dma((2,)),
            dma((3,)),
            dma((groups, 3)),
            dma((4,)),
            dma((4, half)),
            dma((2,)),
        ],
        compiler_params=pltpu.CompilerParams(
            collective_id=0, has_side_effects=True, vmem_limit_bytes=56 * 1024 * 1024
        ),
        cost_estimate=pl.CostEstimate(
            flops=22 * 2 * count * height * 4 * height * width,
            bytes_accessed=2 * tiles.size * 2,
            transcendentals=0,
        ),
    )(tile_rows, keep.T, hand, slot, tiles)


def solution(mesh):
    placed = (P("col", None, "row", None), P("col", None), P("col", None), P("col"))
    return jax.shard_map(
        functools.partial(local, mesh.shape["col"]),
        mesh=mesh,
        in_specs=placed,
        out_specs=P("col", None, "row", None),
        check_vma=False,
    )
```
